512 devices in a mesh: rep: 64 (over y, x, z_lo), ctx: 8 (over z_hi, core).
Axes of the slice: x: 4, y: 8, z: 8 (z_hi: 4, z_lo: 2; z = z_hi * 2 + z_lo), core: 2. Of those that a mesh axis runs over, the one named last changes fastest.
Arguments:
- hidden: bfloat16 [64, 1024, 3584], P('rep', 'ctx'), may hold values from -6 to 6
- queries: bfloat16 [64, 1024, 2048], P('rep', 'ctx'), may hold values from -16 to 16
- values: bfloat16 [64, 1024, 1024], P('rep', 'ctx'), may hold values from -6 to 6
- cotangent: bfloat16 [64, 1024, 2048], P('rep', 'ctx'), may hold values from -6 to 6
- key_weight: bfloat16 [64, 3584, 1024], P('rep', None, 'ctx'), may hold values from -0.09375 to 0.09375
- doc_ids: int32 [64, 1024], P('rep', 'ctx'), may hold values from 0 to 3, never falling along the last dimension, each value on 1 to 512 neighbouring positions
- round_index: int32 [3], replicated, may hold values from 0 to 5
Outputs:
- averaged: bfloat16 [64, 3584, 1024], P('rep', None, 'ctx')
- gradient: bfloat16 [64, 3584, 1024], P('rep', None, 'ctx')
The draws below stay inside these ranges and needn't reach their ends.
Inputs may be any that keep to these rules, and one draw needn't show every extreme that they name: `doc_ids`: document numbers never fall along a replica's positions; each document holds at most 512 positions and one holds exactly that many. `round_index`: the same rounds for every replica.
All inputs are finite; a program needn't handle non-finite values.
Results may differ from the reference program's by a relative error of at most 0.019.
Values may be sent and summed in bfloat16 or wider, within the bound.
A program may use at most 64 MiB of HBM per device.

```python
import math
import jax
import jax.numpy as jnp
import numpy as np
from jax import lax

D = 3584
HDIM = 256
HEADS = 8
KVH = 4
TOK_DEV = 128
DOCS = 4
GOSSIP = 3
REPLICAS = 64
SEQ = 1024
LOG_REP = 6
N_CTX = 8


def block_scale(rng, shape, split, least, largest):
    def one(dim, parts):
        heights = jax.random.uniform(jax.random.fold_in(jax.random.fold_in(rng, 6), dim), (parts,), jnp.float32, least / len(split), largest / len(split))
        return jnp.repeat(jnp.exp(heights), shape[dim] // parts).reshape((-1,) + (1,) * (len(shape) - dim - 1))

    factor_of = one(*split[0])
    for cut in split[1:]:
        factor_of = factor_of * one(*cut)
    return factor_of


def profile(count, total, limit, lean):
    weights = [(1 << 20) // math.isqrt(rank ** lean) + 1 for rank in range(2, count + 1)]
    rest, counts = total - limit - (count - 1), [1] * (count - 1)
    while rest > 0:
        candidates = [i for i in range(count - 1) if counts[i] < limit]
        pool, budget = sum([weights[i] for i in candidates]), rest
        for i in candidates:
            extra = min(limit - counts[i], max(1, budget * weights[i] // pool), rest)
            counts[i] = counts[i] + extra
            rest = rest - extra
    return np.array([limit] + counts)


def ragged_sizes(key, number_of, total, reach, skew):
    if number_of == 2:
        one = jax.random.randint(key, (), max(1, total - reach), min(reach, total - 1) + 1)
        return jnp.stack([one, total - one])
    tallies = jnp.asarray(profile(number_of, total, reach, skew), jnp.int32)
    couples = (number_of - 1) // 2
    source_of, receiver = tallies[1:1 + 2 * couples:2], tallies[2:2 + 2 * couples:2]
    margin = jnp.minimum(source_of - 1, reach - receiver)
    moved = jax.random.randint(jax.random.fold_in(key, 1), (couples,), 0, 1 << 20) % (margin + 1)
    tallies = tallies.at[1:1 + 2 * couples:2].set(source_of - moved).at[2:2 + 2 * couples:2].set(receiver + moved)
    return tallies[jax.random.permutation(jax.random.fold_in(key, 2), number_of)]


def centred(stream_key, shape, deviation, limit, shards=(), kind=jnp.bfloat16):
    gain = block_scale(stream_key, shape, shards, -0.22, 0.18) if shards else 1.0
    array = jax.random.normal(stream_key, shape, jnp.float32) * deviation * gain
    return jnp.minimum(jnp.maximum(array, -limit), limit).astype(kind)


def setup_inputs(seed: int = 0) -> dict:
    seeds = jax.random.split(jax.random.key(seed), 8)
    hidden = centred(seeds[0], (REPLICAS, SEQ, D), 1.0, 6.0, ((0, 64), (1, 8)))
    queries = centred(seeds[1], (REPLICAS, SEQ, HEADS * HDIM), 4.0, 16.0, ((0, 64), (1, 8)))
    values = centred(seeds[2], (REPLICAS, SEQ, KVH * HDIM), 1.0, 6.0, ((0, 64), (1, 8)))
    cotangent = centred(seeds[3], (REPLICAS, SEQ, HEADS * HDIM), 1.0, 6.0, ((0, 64), (1, 8)))
    key_weight = centred(seeds[4], (REPLICAS, D, KVH * HDIM), D ** -0.5, 0.09375, ((0, 64), (2, 8)))
    doc_ids = jax.vmap(lambda own: jnp.searchsorted(jnp.cumsum(ragged_sizes(own, DOCS, SEQ, SEQ // 2, 0)), jnp.arange(SEQ), side="right"))(jax.random.split(seeds[5], REPLICAS)).reshape((REPLICAS, SEQ)).astype(jnp.int32)
    round_index = jax.random.randint(seeds[6], (GOSSIP,), 0, LOG_REP).astype(jnp.int32)
    return {"hidden": hidden, "queries": queries, "values": values, "cotangent": cotangent, "key_weight": key_weight, "doc_ids": doc_ids, "round_index": round_index}


softcap = 50.0
step_size = 0.0005


def attend_block(query_block, block_docs, block_start, key_rows, every_values, every_docs, cot_block):
    tokens = query_block.shape[0]
    key_count = key_rows.shape[0]
    per_group = HEADS // KVH
    score_scale = 1.0 / (HDIM ** 0.5)
    query_heads = query_block.astype(jnp.float32).reshape(tokens, KVH, per_group, HDIM)
    key_heads = key_rows.astype(jnp.float32).reshape(key_count, KVH, HDIM)
    value_heads = every_values.astype(jnp.float32).reshape(key_count, KVH, HDIM)
    cot_heads = cot_block.astype(jnp.float32).reshape(tokens, KVH, per_group, HDIM)
    scores = jnp.einsum('igrd,jgd->grij', query_heads, key_heads) * score_scale
    tanh_part = jnp.tanh(scores / softcap)
    capped = softcap * tanh_part
    query_pos = block_start + jnp.arange(tokens, dtype=jnp.int32)
    columns = jnp.arange(key_count, dtype=jnp.int32)
    allowed = (columns[None, :] <= query_pos[:, None]) & (every_docs[None, :] == block_docs[:, None])
    weighted = jnp.where(allowed, jnp.exp(capped), jnp.zeros_like(capped))
    attention = weighted / jnp.sum(weighted, axis=-1, keepdims=True)
    attention_low = lax.optimization_barrier(attention.astype(jnp.bfloat16)).astype(jnp.float32)
    attended = jnp.einsum('grij,jgd->igrd', attention_low, value_heads)
    row_dot = jnp.einsum('igrd,igrd->gri', cot_heads, attended)
    prob_grad = jnp.einsum('igrd,jgd->grij', cot_heads, value_heads)
    score_grad = attention * (prob_grad - row_dot[..., None]) * (1.0 - tanh_part * tanh_part)
    score_grad = lax.optimization_barrier(score_grad.astype(jnp.bfloat16)).astype(jnp.float32)
    key_terms = jnp.einsum('grij,igrd->jgd', score_grad, query_heads) * score_scale
    return key_terms.reshape(key_count, KVH * HDIM)


def one_replica(hidden, queries, values, cotangent, key_weight, doc_ids):
    key_rows = jnp.dot(hidden, key_weight, preferred_element_type=jnp.float32).astype(jnp.bfloat16)
    query_blocks = queries.reshape(N_CTX, TOK_DEV, HEADS * HDIM)
    cot_blocks = cotangent.reshape(N_CTX, TOK_DEV, HEADS * HDIM)
    doc_blocks = doc_ids.reshape(N_CTX, TOK_DEV)

    def one_block(pieces):
        query_block, block_docs, cot_block, block_index = pieces
        key_terms = attend_block(query_block, block_docs, block_index * TOK_DEV, key_rows, values, doc_ids, cot_block)
        return lax.optimization_barrier(key_terms.astype(jnp.bfloat16)).astype(jnp.float32)

    partials = lax.map(one_block, (query_blocks, doc_blocks, cot_blocks, jnp.arange(N_CTX, dtype=jnp.int32)))
    key_grad = jnp.sum(partials, axis=0).astype(jnp.bfloat16)
    weight_grad = jnp.dot(hidden.T, key_grad, preferred_element_type=jnp.float32)
    stepped = (key_weight.astype(jnp.float32) - step_size * weight_grad).astype(jnp.bfloat16)
    return stepped, weight_grad.astype(jnp.bfloat16)


def reference(hidden, queries, values, cotangent, key_weight, doc_ids, round_index):
    def replica_step(replica_items):
        return one_replica(*replica_items)

    stepped, gradient = lax.map(replica_step, (hidden, queries, values, cotangent, key_weight, doc_ids))
    replica_count = stepped.shape[0]
    replica_ids = jnp.arange(replica_count, dtype=jnp.int32)
    averaged = stepped
    for turn in range(GOSSIP):
        partner_index = jnp.bitwise_xor(replica_ids, jnp.left_shift(jnp.int32(1), round_index[turn]))
        partner = averaged[partner_index]
        averaged = (0.5 * (averaged.astype(jnp.float32) + partner.astype(jnp.float32))).astype(jnp.bfloat16)
    return (averaged, gradient)
```

```python
from functools import partial

import jax
import jax.numpy as jnp
from jax import lax
from jax.experimental import pallas as pl
from jax.experimental.pallas import tpu as pltpu
from jax.sharding import PartitionSpec as P

MESH = pl.DeviceIdType.MESH

HDIM = 256
HEADS = 8
KVH = 4
GOSSIP = 3
N_CTX = 8
CHIPS = 4
ROWS = 128
CHUNKS = 4

softcap = 50.0
step_size = 0.0005


def swapped(x, axis, apart):
    return lax.ppermute(x, axis, [(i, i ^ 1 << apart) for i in range(lax.axis_size(axis))])


def round_partner(payload, round_number, rounds):
    branches = [partial(swapped, axis="rep", apart=level_bit) for level_bit in range(rounds)]
    return lax.switch(round_number, branches, payload)


def nt(a, b):
    return lax.dot_general(a, b, (((1,), (1,)), ((), ())), preferred_element_type=jnp.float32)


def gradient_kernel(
    hid, qry, val, cot, wgt, docs, grad, stepped,
    hall, qall, call, vall, dall, wown, kbuf, dkacc, dksend, dkrecv, dkown,
    local, h_recv, h_send, q_recv, q_send, c_recv, c_send, v_recv, v_send, d_recv, d_send,
    k_recv, k_send, g_recv, g_send,
):
    me = lax.axis_index("ctx")
    chip = me // 2
    core = lax.rem(me, 2)
    sib = chip * 2 + (1 - core)
    up_chip = lax.rem(chip + 1, CHIPS)
    dn_chip = lax.rem(chip + 3, CHIPS)
    opp_chip = lax.rem(chip + 2, CHIPS)
    up = up_chip * 2 + core
    dn = dn_chip * 2 + core
    opp = opp_chip * 2 + core
    rows_of = ROWS // CHUNKS

    def send(src, dst, ssem, rsem, dev):
        return pltpu.make_async_remote_copy(
            src_ref=src, dst_ref=dst, send_sem=ssem, recv_sem=rsem,
            device_id={"ctx": dev}, device_id_type=MESH,
        )

    barrier = pltpu.get_barrier_semaphore()
    for other in range(1, N_CTX):
        pl.semaphore_signal(
            barrier, inc=1, device_id={"ctx": lax.rem(me + other, N_CTX)}, device_id_type=MESH
        )

    head = pl.ds(pl.multiple_of(me * HDIM, HDIM), HDIM)
    kv_head = pl.ds(pl.multiple_of(chip * HDIM, HDIM), HDIM)
    own_half = pl.ds(pl.multiple_of(core * 128, 128), 128)
    sib_half = pl.ds(pl.multiple_of((1 - core) * 128, 128), 128)
    local_copies = [
        pltpu.make_async_copy(hid, hall.at[me], local.at[0]),
        pltpu.make_async_copy(wgt, wown, local.at[1]),
        pltpu.make_async_copy(qry.at[:, head], qall.at[me], local.at[2]),
        pltpu.make_async_copy(cot.at[:, head], call.at[me], local.at[3]),
        pltpu.make_async_copy(val.at[:, kv_head], vall.at[me], local.at[4]),
    ]
    for copy in local_copies:
        copy.start()
    pl.semaphore_wait(barrier, N_CTX - 1)

    started = []

    def go(copy):
        copy.start()
        started.append(copy)

    def piece(k):
        return pl.ds(k * rows_of, rows_of)

    low = list(range(CHUNKS // 2))
    high = list(range(CHUNKS // 2, CHUNKS))

    def h_to(dev, origin, k, sem, src=None):
        slot = hall.at[origin, piece(k), :]
        go(send(slot if src is None else src, slot, h_send.at[sem], h_recv.at[origin, k], dev))

    def h_wait(origin, k):
        slot = hall.at[origin, piece(k), :]
        send(slot, slot, h_send.at[0], h_recv.at[origin, k], sib).wait_recv()

    for a, b in zip(low + high, high + low):
        h_to(up, me, a, a, hid.at[piece(a), :])
        h_to(dn, me, b, CHUNKS + b, hid.at[piece(b), :])
    for k in range(CHUNKS):
        h_to(sib, me, k, 2 * CHUNKS + k, hid.at[piece(k), :])
    go_docs = []
    for other in range(1, N_CTX):
        dev = lax.rem(me + other, N_CTX)
        go(send(docs, dall.at[me], d_send.at[other], d_recv.at[me], dev))
    dall[me] = docs[...]

    sem = 3 * CHUNKS
    for a, b in zip(low, high):
        h_wait(dn, a)
        h_to(up, dn, a, sem, None)
        h_to(sib, dn, a, sem + 1, None)
        h_wait(up, b)
        h_to(dn, up, b, sem + 2, None)
        h_to(sib, up, b, sem + 3, None)
        sem += 4

    for i, (far_chip, far) in enumerate(((up_chip, up), (dn_chip, dn), (opp_chip, opp))):
        for j in range(2):
            dev = far_chip * 2 + j
            feats = pl.ds(pl.multiple_of(dev * HDIM, HDIM), HDIM)
            go(send(qry.at[:, feats], qall.at[me], q_send.at[2 * i + j], q_recv.at[me], dev))
            go(send(cot.at[:, feats], call.at[me], c_send.at[2 * i + j], c_recv.at[me], dev))
        feats = pl.ds(pl.multiple_of(far_chip * HDIM, HDIM), HDIM)
        go(send(val.at[:, feats], vall.at[me], v_send.at[i], v_recv.at[me], far))
    sib_feats = pl.ds(pl.multiple_of(sib * HDIM, HDIM), HDIM)
    go(send(qry.at[:, sib_feats], qall.at[me], q_send.at[6], q_recv.at[me], sib))
    go(send(cot.at[:, sib_feats], call.at[me], c_send.at[6], c_recv.at[me], sib))
    go(send(val.at[:, kv_head], vall.at[me], v_send.at[3], v_recv.at[me], sib))

    for copy in local_copies:
        copy.wait()

    def project(p):
        block = hall[pl.ds(2 * p, 2)].reshape(2 * ROWS, hall.shape[2])
        out = jnp.dot(block, wown[...], preferred_element_type=jnp.float32)
        rows = pl.ds(pl.multiple_of(p * 2 * ROWS, 2 * ROWS), 2 * ROWS)
        kbuf[rows, own_half] = out.astype(jnp.bfloat16)
        go(send(kbuf.at[rows, own_half], kbuf.at[rows, own_half], k_send.at[p], k_recv.at[p], sib))

    for k in range(CHUNKS):
        h_wait(sib, k)
    project(chip)

    for a, b in zip(high, low):
        h_wait(dn, a)
        h_to(sib, dn, a, sem, None)
        h_wait(up, b)
        h_to(sib, up, b, sem + 1, None)
        sem += 2
    for k in range(CHUNKS):
        h_wait(up_chip * 2 + 1 - core, k)
    project(up_chip)
    for k in range(CHUNKS):
        h_wait(dn_chip * 2 + 1 - core, k)
    project(dn_chip)
    for a, b in zip(low, high):
        h_wait(opp, a)
        h_to(sib, opp, a, sem, None)
        h_wait(opp, b)
        h_to(sib, opp, b, sem + 1, None)
        sem += 2
    for k in range(CHUNKS):
        h_wait(opp_chip * 2 + 1 - core, k)
    project(opp_chip)

    for i, far in enumerate((up, dn, opp)):
        send(vall.at[far], vall.at[far], v_send.at[0], v_recv.at[far], sib).wait_recv()
        go(send(vall.at[far], vall.at[far], v_send.at[4 + i], v_recv.at[far], sib))
    for other in range(1, N_CTX):
        src = lax.rem(me + other, N_CTX)
        send(qall.at[src], qall.at[src], q_send.at[0], q_recv.at[src], sib).wait_recv()
        send(call.at[src], call.at[src], c_send.at[0], c_recv.at[src], sib).wait_recv()
        send(docs, dall.at[src], d_send.at[0], d_recv.at[src], sib).wait_recv()
    for p in (chip, up_chip, dn_chip, opp_chip):
        src = 2 * p + 1 - core
        send(vall.at[src], vall.at[src], v_send.at[0], v_recv.at[src], sib).wait_recv()
        rows = pl.ds(pl.multiple_of(p * 2 * ROWS, 2 * ROWS), 2 * ROWS)
        half = kbuf.at[rows, sib_half]
        send(half, half, k_send.at[0], k_recv.at[p], sib).wait_recv()

    doc_rows = [dall[s] for s in range(N_CTX)]
    starts = [jnp.zeros(row.shape, jnp.float32) for row in doc_rows]
    for v in range(3):
        total = jnp.zeros((1, 1), jnp.float32)
        for row in doc_rows:
            total = total + jnp.sum(jnp.where(row == v, 1.0, 0.0), axis=1, keepdims=True)
        starts = [s + jnp.where(row > v, total, 0.0) for s, row in zip(starts, doc_rows)]

    dkacc[...] = jnp.zeros_like(dkacc)
    block = 2 * ROWS
    for p in range(CHIPS):
        first = max(p - 2, 0)
        keys = (p + 1 - first) * block
        rows = pl.ds(first * block, keys)
        q = qall[2 * p : 2 * p + 2].reshape(block, HDIM)
        c = call[2 * p : 2 * p + 2].reshape(block, HDIM)
        v = vall[2 * first : 2 * p + 2].reshape(keys, HDIM)
        start = jnp.concatenate([starts[2 * p], starts[2 * p + 1]], axis=1).astype(jnp.int32)
        t = jnp.tanh(nt(kbuf[rows, :], q) * (1.0 / (HDIM**0.5 * softcap)))
        key_pos = first * block + lax.broadcasted_iota(jnp.int32, (keys, block), 0)
        query_pos = p * block + lax.broadcasted_iota(jnp.int32, (keys, block), 1)
        allowed = (key_pos <= query_pos) & (key_pos >= start)
        e = jnp.where(allowed, jnp.exp(softcap * t), 0.0)
        prob_grad = nt(v, c)
        norm = 1.0 / jnp.sum(e, axis=0, keepdims=True)
        row_dot = jnp.sum(e * prob_grad, axis=0, keepdims=True) * norm
        score_grad = (e * norm) * (prob_grad - row_dot) * (1.0 - t * t)
        dkacc[rows, :] += jnp.dot(
            score_grad.astype(jnp.bfloat16), q, preferred_element_type=jnp.float32
        )

    scale = 1.0 / HDIM**0.5
    dksend[...] = (dkacc[:, sib_half] * scale).astype(jnp.bfloat16)
    swap = send(dksend, dkrecv, g_send.at[0], g_recv.at[0], sib)
    go(swap)
    swap.wait_recv()
    dk = dkacc[:, own_half] * scale + dkrecv[...].astype(jnp.float32)
    dkown[...] = dk.T.astype(jnp.bfloat16)

    width = 512

    @pl.loop(0, grad.shape[0] // width)
    def _(i):
        cols = pl.ds(pl.multiple_of(i * width, width), width)
        h = hall[:, :, cols].reshape(N_CTX * ROWS, width)
        g = jnp.dot(dkown[...], h, preferred_element_type=jnp.float32).T
        grad[cols, :] = g.astype(jnp.bfloat16)
        stepped[cols, :] = (wown[cols, :].astype(jnp.float32) - step_size * g).astype(jnp.bfloat16)

    for copy in started:
        copy.wait_send()


def local_gradient(hidden, queries, values, cotangent, key_weight, doc_ids):
    depth = hidden.shape[1]
    dma = pltpu.SemaphoreType.DMA
    bf16, f32 = jnp.bfloat16, jnp.float32
    any_spec = pl.BlockSpec(memory_space=pl.ANY)
    vmem = pl.BlockSpec(memory_space=pltpu.VMEM)
    seq = N_CTX * ROWS
    return pl.pallas_call(
        gradient_kernel,
        out_shape=[jax.ShapeDtypeStruct((depth, 128), bf16)] * 2,
        in_specs=[any_spec] * 5 + [vmem],
        out_specs=[vmem] * 2,
        scratch_shapes=[
            pltpu.VMEM((N_CTX, ROWS, depth), bf16),
            pltpu.VMEM((N_CTX, ROWS, HDIM), bf16),
            pltpu.VMEM((N_CTX, ROWS, HDIM), bf16),
            pltpu.VMEM((N_CTX, ROWS, HDIM), bf16),
            pltpu.VMEM((N_CTX, 1, ROWS), jnp.int32),
            pltpu.VMEM((depth, 128), bf16),
            pltpu.VMEM((seq, HDIM), bf16),
            pltpu.VMEM((seq, HDIM), f32),
            pltpu.VMEM((seq, 128), bf16),
            pltpu.VMEM((seq, 128), bf16),
            pltpu.VMEM((128, seq), bf16),
            dma((5,)),
            dma((N_CTX, CHUNKS)),
            dma((7 * CHUNKS,)),
            dma((N_CTX,)),
            dma((7,)),
            dma((N_CTX,)),
            dma((7,)),
            dma((N_CTX,)),
            dma((7,)),
            dma((N_CTX,)),
            dma((N_CTX,)),
            dma((CHIPS,)),
            dma((CHIPS,)),
            dma((1,)),
            dma((1,)),
        ],
        compiler_params=pltpu.CompilerParams(
            collective_id=0, has_side_effects=True, vmem_limit_bytes=48 * 1024 * 1024
        ),
        name="gradient",
    )(hidden, queries, values, cotangent, key_weight, doc_ids)


def on_device(hidden, queries, values, cotangent, key_weight, doc_ids, round_index):
    rounds = lax.axis_size("rep").bit_length() - 1
    gradient, averaged = local_gradient(
        hidden[0], queries[0], values[0], cotangent[0], key_weight[0], doc_ids
    )
    for turn in range(GOSSIP):
        partner = round_partner(averaged, round_index[turn], rounds)
        averaged = (0.5 * (averaged.astype(jnp.float32) + partner.astype(jnp.float32))).astype(
            jnp.bfloat16
        )
    return (averaged[None], gradient[None])


def solution(mesh):
    return jax.shard_map(
        on_device,
        mesh=mesh,
        in_specs=(
            P("rep", "ctx", None),
            P("rep", "ctx", None),
            P("rep", "ctx", None),
            P("rep", "ctx", None),
            P("rep", None, "ctx"),
            P("rep", "ctx"),
            P(),
        ),
        out_specs=(P("rep", None, "ctx"), P("rep", None, "ctx")),
        check_vma=False,
    )
```

```python
import itertools
from functools import partial

import jax
import jax.numpy as jnp
from jax import lax
from jax.experimental import pallas as pl
from jax.experimental.pallas import tpu as pltpu
from jax.sharding import PartitionSpec as P

MESH = pl.DeviceIdType.MESH

HDIM = 256
HEADS = 8
KVH = 4
GOSSIP = 3
N_CTX = 8
CHIPS = 4
ROWS = 128
CHUNKS = 4
RANKS = 6

softcap = 50.0
step_size = 0.0005


ROUTE = (("z", 1), ("x", 1), ("x", 1), ("y", 1), ("y", 2), ("y", 2))
PIECES = 7


def round_orders(bits):
    load = {"x": 0.0, "y": 0.0, "z": 0.0}
    orders = []
    for _ in range(PIECES):
        best = None
        for order in itertools.permutations(bits):
            after = dict(load)
            for level, bit in enumerate(order):
                axis, hops = ROUTE[bit]
                after[axis] += hops * 0.5**level
            key = (max(after.values()), sum(after.values()), order)
            if best is None or key < best[0]:
                best = (key, order, after)
        orders.append(best[1])
        load = best[2]
    return orders


def gossip_kernel(bits, x, out, acc, first, second, third, send_sem, recv_sem):
    me = lax.axis_index("rep")
    count = len(bits)
    landing = (first, second, third)
    digit = {bit: lax.rem(me // (1 << bit), 2) for bit in bits}
    partner = {bit: me + (1 - 2 * digit[bit]) * (1 << bit) for bit in bits}
    barrier = pltpu.get_barrier_semaphore()
    for bit in bits:
        pl.semaphore_signal(barrier, inc=1, device_id={"rep": partner[bit]}, device_id_type=MESH)
    pl.semaphore_wait(barrier, count)

    rows = x.shape[0] // PIECES
    stages = 2 * count - 1
    orders = round_orders(bits)

    def region(piece, level):
        base, size = piece * rows, rows
        for bit in orders[piece][:level]:
            size //= 2
            base = base + digit[bit] * size
        return base, size

    def at(ref, base, size):
        start = base if isinstance(base, int) else pl.multiple_of(base, 32)
        return ref.at[pl.ds(start, size), :]

    def transfer(piece, stage, arriving=False):
        order = orders[piece]
        if stage < count - 1:
            bit = order[stage]
            base, size = region(piece, stage)
            half = size // 2
            src = x if stage == 0 else acc
            away = base + (1 - digit[bit]) * half
            sent, dst = at(src, away, half), at(landing[stage], away, half)
            came = at(landing[stage], base + digit[bit] * half, half)
        elif stage == count - 1:
            bit = order[stage]
            base, size = region(piece, stage)
            src = x if stage == 0 else acc
            sent, dst = at(src, base, size), at(landing[stage], base, size)
            came = dst
        else:
            level = stages - 1 - stage
            bit = order[level]
            base, size = region(piece, level)
            half = size // 2
            sent = at(out, base + digit[bit] * half, half)
            dst = sent
            came = at(out, base + (1 - digit[bit]) * half, half)

        return pltpu.make_async_remote_copy(
            src_ref=sent, dst_ref=came if arriving else dst, send_sem=send_sem.at[piece, stage],
            recv_sem=recv_sem.at[piece, stage], device_id={"rep": partner[bit]},
            device_id_type=MESH,
        )

    def finish(piece, stage):
        transfer(piece, stage, arriving=True).wait_recv()
        if stage < count:
            base, size = region(piece, min(stage + 1, count - 1))
            own = at(x if stage == 0 else acc, base, size)
            other = at(landing[stage], base, size)
            mean = 0.5 * (own[...].astype(jnp.float32) + other[...].astype(jnp.float32))
            at(out if stage == count - 1 else acc, base, size)[...] = mean.astype(jnp.bfloat16)

    for piece in range(PIECES):
        transfer(piece, 0).start()
    for step in range(PIECES + stages - 1):
        for stage in range(stages - 1, -1, -1):
            piece = step - stage
            if 0 <= piece < PIECES:
                finish(piece, stage)
                if stage + 1 < stages:
                    transfer(piece, stage + 1).start()
    for piece in range(PIECES):
        for stage in range(stages):
            transfer(piece, stage).wait_send()


def gossip(bits, number):
    def run(stepped):
        shape = stepped.shape
        stages = 2 * len(bits) - 1
        vmem = pl.BlockSpec(memory_space=pltpu.VMEM)
        return pl.pallas_call(
            partial(gossip_kernel, bits),
            out_shape=jax.ShapeDtypeStruct(shape, jnp.bfloat16),
            in_specs=[vmem],
            out_specs=vmem,
            scratch_shapes=[pltpu.VMEM(shape, jnp.bfloat16)] * 4
            + [pltpu.SemaphoreType.DMA((PIECES, stages))] * 2,
            compiler_params=pltpu.CompilerParams(
                collective_id=number, has_side_effects=True, vmem_limit_bytes=16 * 1024 * 1024
            ),
            name="gossip",
        )(stepped)

    return run


def gossip_rounds(stepped, mask):
    branches = []
    for case in range(1 << RANKS):
        bits = tuple(bit for bit in range(RANKS) if case >> bit & 1)
        if 1 <= len(bits) <= GOSSIP:
            branches.append(gossip(bits, 1 + case))
        else:
            branches.append(lambda kept: kept)
    return lax.switch(mask, branches, stepped)


def nt(a, b):
    return lax.dot_general(a, b, (((1,), (1,)), ((), ())), preferred_element_type=jnp.float32)


def gradient_kernel(
    hid, qry, val, cot, wgt, docs, rounds, grad, stepped, mask,
    hall, qall, call, vall, dall, wown, kbuf, dkacc, dksend, dkrecv, dkown,
    local, h_recv, h_send, q_recv, q_send, c_recv, c_send, v_recv, v_send, d_recv, d_send,
    k_recv, k_send, g_recv, g_send,
):
    me = lax.axis_index("ctx")
    chip = me // 2
    core = lax.rem(me, 2)
    sib = chip * 2 + (1 - core)
    up_chip = lax.rem(chip + 1, CHIPS)
    dn_chip = lax.rem(chip + 3, CHIPS)
    opp_chip = lax.rem(chip + 2, CHIPS)
    up = up_chip * 2 + core
    dn = dn_chip * 2 + core
    opp = opp_chip * 2 + core
    rows_of = ROWS // CHUNKS

    def send(src, dst, ssem, rsem, dev):
        return pltpu.make_async_remote_copy(
            src_ref=src, dst_ref=dst, send_sem=ssem, recv_sem=rsem,
            device_id={"ctx": dev}, device_id_type=MESH,
        )

    mask[0] = (1 << rounds[0]) | (1 << rounds[1]) | (1 << rounds[2])
    barrier = pltpu.get_barrier_semaphore()
    for other in range(1, N_CTX):
        pl.semaphore_signal(
            barrier, inc=1, device_id={"ctx": lax.rem(me + other, N_CTX)}, device_id_type=MESH
        )

    head = pl.ds(pl.multiple_of(me * HDIM, HDIM), HDIM)
    kv_head = pl.ds(pl.multiple_of(chip * HDIM, HDIM), HDIM)
    own_half = pl.ds(pl.multiple_of(core * 128, 128), 128)
    sib_half = pl.ds(pl.multiple_of((1 - core) * 128, 128), 128)
    local_copies = [
        pltpu.make_async_copy(hid, hall.at[me], local.at[0]),
        pltpu.make_async_copy(wgt, wown, local.at[1]),
        pltpu.make_async_copy(qry.at[:, head], qall.at[me], local.at[2]),
        pltpu.make_async_copy(cot.at[:, head], call.at[me], local.at[3]),
        pltpu.make_async_copy(val.at[:, kv_head], vall.at[me], local.at[4]),
    ]
    for copy in local_copies:
        copy.start()
    pl.semaphore_wait(barrier, N_CTX - 1)

    started = []

    def go(copy):
        copy.start()
        started.append(copy)

    def piece(k):
        return pl.ds(k * rows_of, rows_of)

    low = list(range(CHUNKS // 2))
    high = list(range(CHUNKS // 2, CHUNKS))

    def h_to(dev, origin, k, sem, src=None):
        slot = hall.at[origin, piece(k), :]
        go(send(slot if src is None else src, slot, h_send.at[sem], h_recv.at[origin, k], dev))

    def h_wait(origin, k):
        slot = hall.at[origin, piece(k), :]
        send(slot, slot, h_send.at[0], h_recv.at[origin, k], sib).wait_recv()

    for a, b in zip(low + high, high + low):
        h_to(up, me, a, a, hid.at[piece(a), :])
        h_to(dn, me, b, CHUNKS + b, hid.at[piece(b), :])
    for k in range(CHUNKS):
        h_to(sib, me, k, 2 * CHUNKS + k, hid.at[piece(k), :])
    go_docs = []
    for other in range(1, N_CTX):
        dev = lax.rem(me + other, N_CTX)
        go(send(docs, dall.at[me], d_send.at[other], d_recv.at[me], dev))
    dall[me] = docs[...]

    sem = 3 * CHUNKS
    for a, b in zip(low, high):
        h_wait(dn, a)
        h_to(up, dn, a, sem, None)
        h_to(sib, dn, a, sem + 1, None)
        h_wait(up, b)
        h_to(dn, up, b, sem + 2, None)
        h_to(sib, up, b, sem + 3, None)
        sem += 4

    for i, (far_chip, far) in enumerate(((up_chip, up), (dn_chip, dn), (opp_chip, opp))):
        for j in range(2):
            dev = far_chip * 2 + j
            feats = pl.ds(pl.multiple_of(dev * HDIM, HDIM), HDIM)
            go(send(qry.at[:, feats], qall.at[me], q_send.at[2 * i + j], q_recv.at[me], dev))
            go(send(cot.at[:, feats], call.at[me], c_send.at[2 * i + j], c_recv.at[me], dev))
        feats = pl.ds(pl.multiple_of(far_chip * HDIM, HDIM), HDIM)
        go(send(val.at[:, feats], vall.at[me], v_send.at[i], v_recv.at[me], far))
    sib_feats = pl.ds(pl.multiple_of(sib * HDIM, HDIM), HDIM)
    go(send(qry.at[:, sib_feats], qall.at[me], q_send.at[6], q_recv.at[me], sib))
    go(send(cot.at[:, sib_feats], call.at[me], c_send.at[6], c_recv.at[me], sib))
    go(send(val.at[:, kv_head], vall.at[me], v_send.at[3], v_recv.at[me], sib))

    for copy in local_copies:
        copy.wait()

    def project(p):
        block = hall[pl.ds(2 * p, 2)].reshape(2 * ROWS, hall.shape[2])
        out = jnp.dot(block, wown[...], preferred_element_type=jnp.float32)
        rows = pl.ds(pl.multiple_of(p * 2 * ROWS, 2 * ROWS), 2 * ROWS)
        kbuf[rows, own_half] = out.astype(jnp.bfloat16)
        go(send(kbuf.at[rows, own_half], kbuf.at[rows, own_half], k_send.at[p], k_recv.at[p], sib))

    for k in range(CHUNKS):
        h_wait(sib, k)
    project(chip)

    for a, b in zip(high, low):
        h_wait(dn, a)
        h_to(sib, dn, a, sem, None)
        h_wait(up, b)
        h_to(sib, up, b, sem + 1, None)
        sem += 2
    for k in range(CHUNKS):
        h_wait(up_chip * 2 + 1 - core, k)
    project(up_chip)
    for k in range(CHUNKS):
        h_wait(dn_chip * 2 + 1 - core, k)
    project(dn_chip)
    for a, b in zip(low, high):
        h_wait(opp, a)
        h_to(sib, opp, a, sem, None)
        h_wait(opp, b)
        h_to(sib, opp, b, sem + 1, None)
        sem += 2
    for k in range(CHUNKS):
        h_wait(opp_chip * 2 + 1 - core, k)
    project(opp_chip)

    for i, far in enumerate((up, dn, opp)):
        send(vall.at[far], vall.at[far], v_send.at[0], v_recv.at[far], sib).wait_recv()
        go(send(vall.at[far], vall.at[far], v_send.at[4 + i], v_recv.at[far], sib))
    for other in range(1, N_CTX):
        src = lax.rem(me + other, N_CTX)
        send(qall.at[src], qall.at[src], q_send.at[0], q_recv.at[src], sib).wait_recv()
        send(call.at[src], call.at[src], c_send.at[0], c_recv.at[src], sib).wait_recv()
        send(docs, dall.at[src], d_send.at[0], d_recv.at[src], sib).wait_recv()
    for p in (chip, up_chip, dn_chip, opp_chip):
        src = 2 * p + 1 - core
        send(vall.at[src], vall.at[src], v_send.at[0], v_recv.at[src], sib).wait_recv()
        rows = pl.ds(pl.multiple_of(p * 2 * ROWS, 2 * ROWS), 2 * ROWS)
        half = kbuf.at[rows, sib_half]
        send(half, half, k_send.at[0], k_recv.at[p], sib).wait_recv()

    doc_rows = [dall[s] for s in range(N_CTX)]
    starts = [jnp.zeros(row.shape, jnp.float32) for row in doc_rows]
    for v in range(3):
        total = jnp.zeros((1, 1), jnp.float32)
        for row in doc_rows:
            total = total + jnp.sum(jnp.where(row == v, 1.0, 0.0), axis=1, keepdims=True)
        starts = [s + jnp.where(row > v, total, 0.0) for s, row in zip(starts, doc_rows)]

    dkacc[...] = jnp.zeros_like(dkacc)
    block = 2 * ROWS
    for p in range(CHIPS):
        first = max(p - 2, 0)
        keys = (p + 1 - first) * block
        rows = pl.ds(first * block, keys)
        q = qall[2 * p : 2 * p + 2].reshape(block, HDIM)
        c = call[2 * p : 2 * p + 2].reshape(block, HDIM)
        v = vall[2 * first : 2 * p + 2].reshape(keys, HDIM)
        start = jnp.concatenate([starts[2 * p], starts[2 * p + 1]], axis=1).astype(jnp.int32)
        t = jnp.tanh(nt(kbuf[rows, :], q) * (1.0 / (HDIM**0.5 * softcap)))
        key_pos = first * block + lax.broadcasted_iota(jnp.int32, (keys, block), 0)
        query_pos = p * block + lax.broadcasted_iota(jnp.int32, (keys, block), 1)
        allowed = (key_pos <= query_pos) & (key_pos >= start)
        e = jnp.where(allowed, jnp.exp(softcap * t), 0.0)
        prob_grad = nt(v, c)
        norm = 1.0 / jnp.sum(e, axis=0, keepdims=True)
        row_dot = jnp.sum(e * prob_grad, axis=0, keepdims=True) * norm
        score_grad = (e * norm) * (prob_grad - row_dot) * (1.0 - t * t)
        dkacc[rows, :] += jnp.dot(
            score_grad.astype(jnp.bfloat16), q, preferred_element_type=jnp.float32
        )

    scale = 1.0 / HDIM**0.5
    dksend[...] = (dkacc[:, sib_half] * scale).astype(jnp.bfloat16)
    swap = send(dksend, dkrecv, g_send.at[0], g_recv.at[0], sib)
    go(swap)
    swap.wait_recv()
    dk = dkacc[:, own_half] * scale + dkrecv[...].astype(jnp.float32)
    dkown[...] = dk.T.astype(jnp.bfloat16)

    width = 512

    @pl.loop(0, grad.shape[0] // width)
    def _(i):
        cols = pl.ds(pl.multiple_of(i * width, width), width)
        h = hall[:, :, cols].reshape(N_CTX * ROWS, width)
        g = jnp.dot(dkown[...], h, preferred_element_type=jnp.float32).T
        grad[cols, :] = g.astype(jnp.bfloat16)
        stepped[cols, :] = (wown[cols, :].astype(jnp.float32) - step_size * g).astype(jnp.bfloat16)

    for copy in started:
        copy.wait_send()


def local_gradient(hidden, queries, values, cotangent, key_weight, doc_ids, round_index):
    depth = hidden.shape[1]
    dma = pltpu.SemaphoreType.DMA
    bf16, f32 = jnp.bfloat16, jnp.float32
    hbm = pl.BlockSpec(memory_space=pltpu.HBM)
    smem = pl.BlockSpec(memory_space=pltpu.SMEM)
    vmem = pl.BlockSpec(memory_space=pltpu.VMEM)
    seq = N_CTX * ROWS
    return pl.pallas_call(
        gradient_kernel,
        out_shape=[jax.ShapeDtypeStruct((depth, 128), bf16)] * 2
        + [jax.ShapeDtypeStruct((1,), jnp.int32)],
        in_specs=[hbm] * 5 + [vmem, smem],
        out_specs=[vmem, vmem, smem],
        scratch_shapes=[
            pltpu.VMEM((N_CTX, ROWS, depth), bf16),
            pltpu.VMEM((N_CTX, ROWS, HDIM), bf16),
            pltpu.VMEM((N_CTX, ROWS, HDIM), bf16),
            pltpu.VMEM((N_CTX, ROWS, HDIM), bf16),
            pltpu.VMEM((N_CTX, 1, ROWS), jnp.int32),
            pltpu.VMEM((depth, 128), bf16),
            pltpu.VMEM((seq, HDIM), bf16),
            pltpu.VMEM((seq, HDIM), f32),
            pltpu.VMEM((seq, 128), bf16),
            pltpu.VMEM((seq, 128), bf16),
            pltpu.VMEM((128, seq), bf16),
            dma((5,)),
            dma((N_CTX, CHUNKS)),
            dma((7 * CHUNKS,)),
            dma((N_CTX,)),
            dma((7,)),
            dma((N_CTX,)),
            dma((7,)),
            dma((N_CTX,)),
            dma((7,)),
            dma((N_CTX,)),
            dma((N_CTX,)),
            dma((CHIPS,)),
            dma((CHIPS,)),
            dma((1,)),
            dma((1,)),
        ],
        compiler_params=pltpu.CompilerParams(
            collective_id=0, has_side_effects=True, vmem_limit_bytes=48 * 1024 * 1024
        ),
        name="gradient",
    )(hidden, queries, values, cotangent, key_weight, doc_ids, round_index)


def on_device(hidden, queries, values, cotangent, key_weight, doc_ids, round_index):
    gradient, stepped, mask = local_gradient(
        hidden[0], queries[0], values[0], cotangent[0], key_weight[0], doc_ids, round_index
    )
    averaged = gossip_rounds(stepped, mask[0])
    return (averaged[None], gradient[None])


def solution(mesh):
    return jax.shard_map(
        on_device,
        mesh=mesh,
        in_specs=(
            P("rep", "ctx", None),
            P("rep", "ctx", None),
            P("rep", "ctx", None),
            P("rep", "ctx", None),
            P("rep", None, "ctx"),
            P("rep", "ctx"),
            P(),
        ),
        out_specs=(P("rep", None, "ctx"), P("rep", None, "ctx")),
        check_vma=False,
    )
```

```python
from functools import partial

import jax
import jax.numpy as jnp
from jax import lax
from jax.experimental import pallas as pl
from jax.experimental.pallas import tpu as pltpu
from jax.sharding import PartitionSpec as P

MESH = pl.DeviceIdType.MESH

HDIM = 256
HEADS = 8
KVH = 4
GOSSIP = 3
N_CTX = 8
CHIPS = 4
ROWS = 128
CHUNKS = 4
RANKS = 6

softcap = 50.0
step_size = 0.0005


PIECES = 7
INNER = 3


def gossip_plan(bits):
    outer = tuple(bit for bit in bits if bit < INNER)
    inner = tuple(bit for bit in bits if bit >= INNER)
    if not (outer and inner):
        outer, inner = (), bits
    depth = 1 if outer else 0
    if len(inner) == 1:
        plan = [("swap", inner, depth)]
    else:
        plan = [("scatter", inner, depth), ("gather", inner, depth)]
    if outer:
        plan = [("scatter", outer, 0)] + plan + [("gather", outer, 0)]
    return plan


def gossip_kernel(bits, x, out, acc, landing, send_sem, recv_sem):
    me = lax.axis_index("rep")
    plan = gossip_plan(bits)
    stages = len(plan)
    reduced = max(s for s, (kind, _, _) in enumerate(plan) if kind != "gather")
    rows = x.shape[0] // PIECES
    digit = {bit: lax.rem(me // (1 << bit), 2) for bit in bits}

    def peers(group):
        place = sum(digit[bit] << i for i, bit in enumerate(group))
        others = []
        for flip in range(1, 1 << len(group)):
            device, there = me, 0
            for i, bit in enumerate(group):
                if flip >> i & 1:
                    device = device + (1 - 2 * digit[bit]) * (1 << bit)
                    there = there + ((1 - digit[bit]) << i)
                else:
                    there = there + (digit[bit] << i)
            others.append((device, there))
        return place, others

    groups = {group: peers(group) for _, group, _ in plan}
    met = [device for _, others in groups.values() for device, _ in others]
    barrier = pltpu.get_barrier_semaphore()
    for device in met:
        pl.semaphore_signal(barrier, inc=1, device_id={"rep": device}, device_id_type=MESH)
    pl.semaphore_wait(barrier, len(met))

    def region(piece, depth):
        base, size = piece * rows, rows
        if depth:
            group = plan[0][1]
            size //= 1 << len(group)
            base = base + groups[group][0] * size
        return base, size

    def at(ref, base, size):
        start = base if isinstance(base, int) else pl.multiple_of(base, 16)
        return ref.at[pl.ds(start, size), :]

    def landed(stage, slot, piece, size):
        return landing.at[stage, slot, pl.ds(piece * size, size), :]

    def transfers(piece, stage, arriving=False):
        kind, group, depth = plan[stage]
        base, size = region(piece, depth)
        src = x if stage == 0 else acc
        place, others = groups[group]
        part = size if kind == "swap" else size >> len(group)
        for slot, (device, there) in enumerate(others):
            if kind == "gather":
                sent = at(out, base + place * part, part)
                dst = at(out, base + there * part, part) if arriving else sent
            else:
                sent = at(src, base if kind == "swap" else base + there * part, part)
                dst = landed(stage, slot, piece, part)
            yield pltpu.make_async_remote_copy(
                src_ref=sent, dst_ref=dst, send_sem=send_sem.at[piece, stage, slot],
                recv_sem=recv_sem.at[piece, stage, slot], device_id={"rep": device},
                device_id_type=MESH,
            )

    def start(piece, stage):
        for copy in transfers(piece, stage):
            copy.start()

    def finish(piece, stage):
        for copy in transfers(piece, stage, arriving=True):
            copy.wait_recv()
        kind, group, depth = plan[stage]
        if kind != "gather":
            base, size = region(piece, depth)
            place, others = groups[group]
            if kind == "scatter":
                size >>= len(group)
                base = base + place * size
            total = at(x if stage == 0 else acc, base, size)[...].astype(jnp.float32)
            for slot in range(len(others)):
                total = total + landed(stage, slot, piece, size)[...].astype(jnp.float32)
            mean = total * (1.0 / (1 << len(group)))
            at(out if stage == reduced else acc, base, size)[...] = mean.astype(jnp.bfloat16)

    for piece in range(PIECES):
        start(piece, 0)
    for stage in range(stages):
        for piece in range(PIECES):
            finish(piece, stage)
            if stage + 1 < stages:
                start(piece, stage + 1)
    for piece in range(PIECES):
        for stage in range(stages):
            for copy in transfers(piece, stage):
                copy.wait_send()


def gossip(bits, number):
    def run(stepped):
        shape = stepped.shape
        plan = gossip_plan(bits)
        sums = [s for s, (kind, _, _) in enumerate(plan) if kind != "gather"]
        slots = max((1 << len(group)) - 1 for _, group, _ in plan)
        deepest = max(shape[0] >> (0 if kind == "swap" else len(group)) for kind, group, _ in plan)
        vmem = pl.BlockSpec(memory_space=pltpu.VMEM)
        return pl.pallas_call(
            partial(gossip_kernel, bits),
            out_shape=jax.ShapeDtypeStruct(shape, jnp.bfloat16),
            in_specs=[vmem],
            out_specs=vmem,
            scratch_shapes=[
                pltpu.VMEM(shape, jnp.bfloat16),
                pltpu.VMEM((max(sums) + 1, slots, deepest, shape[1]), jnp.bfloat16),
            ]
            + [pltpu.SemaphoreType.DMA((PIECES, len(plan), slots))] * 2,
            compiler_params=pltpu.CompilerParams(
                collective_id=number, has_side_effects=True, vmem_limit_bytes=24 * 1024 * 1024
            ),
            name="gossip",
        )(stepped)

    return run


def gossip_rounds(stepped, mask):
    branches = []
    for case in range(1 << RANKS):
        bits = tuple(bit for bit in range(RANKS) if case >> bit & 1)
        if 1 <= len(bits) <= GOSSIP:
            branches.append(gossip(bits, 1 + case))
        else:
            branches.append(lambda kept: kept)
    return lax.switch(mask, branches, stepped)


def nt(a, b):
    return lax.dot_general(a, b, (((1,), (1,)), ((), ())), preferred_element_type=jnp.float32)


def gradient_kernel(
    hid, qry, val, cot, wgt, docs, rounds, grad, stepped, mask,
    hall, qall, call, vall, dall, wown, kbuf, dkacc, dksend, dkrecv, dkown,
    local, h_recv, h_send, q_recv, q_send, c_recv, c_send, v_recv, v_send, d_recv, d_send,
    k_recv, k_send, g_recv, g_send,
):
    me = lax.axis_index("ctx")
    chip = me // 2
    core = lax.rem(me, 2)
    sib = chip * 2 + (1 - core)
    up_chip = lax.rem(chip + 1, CHIPS)
    dn_chip = lax.rem(chip + 3, CHIPS)
    opp_chip = lax.rem(chip + 2, CHIPS)
    up = up_chip * 2 + core
    dn = dn_chip * 2 + core
    opp = opp_chip * 2 + core
    rows_of = ROWS // CHUNKS

    def send(src, dst, ssem, rsem, dev):
        return pltpu.make_async_remote_copy(
            src_ref=src, dst_ref=dst, send_sem=ssem, recv_sem=rsem,
            device_id={"ctx": dev}, device_id_type=MESH,
        )

    mask[0] = (1 << rounds[0]) | (1 << rounds[1]) | (1 << rounds[2])
    barrier = pltpu.get_barrier_semaphore()
    for other in (sib, up, dn):
        pl.semaphore_signal(barrier, inc=1, device_id={"ctx": other}, device_id_type=MESH)

    head = pl.ds(pl.multiple_of(me * HDIM, HDIM), HDIM)
    kv_head = pl.ds(pl.multiple_of(chip * HDIM, HDIM), HDIM)
    own_half = pl.ds(pl.multiple_of(core * 128, 128), 128)
    sib_half = pl.ds(pl.multiple_of((1 - core) * 128, 128), 128)
    local_copies = [
        pltpu.make_async_copy(hid, hall.at[me], local.at[0]),
        pltpu.make_async_copy(wgt, wown, local.at[1]),
        pltpu.make_async_copy(qry.at[:, head], qall.at[me], local.at[2]),
        pltpu.make_async_copy(cot.at[:, head], call.at[me], local.at[3]),
        pltpu.make_async_copy(val.at[:, kv_head], vall.at[me], local.at[4]),
    ]
    for copy in local_copies:
        copy.start()
    pl.semaphore_wait(barrier, 3)

    started = []

    def go(copy):
        copy.start()
        started.append(copy)

    def piece(k):
        return pl.ds(k * rows_of, rows_of)

    low = list(range(CHUNKS // 2))
    high = list(range(CHUNKS // 2, CHUNKS))

    def h_to(dev, origin, k, sem, src=None):
        slot = hall.at[origin, piece(k), :]
        go(send(slot if src is None else src, slot, h_send.at[sem], h_recv.at[origin, k], dev))

    def h_wait(origin, k):
        slot = hall.at[origin, piece(k), :]
        send(slot, slot, h_send.at[0], h_recv.at[origin, k], sib).wait_recv()

    for a, b in zip(low + high, high + low):
        h_to(up, me, a, a, hid.at[piece(a), :])
        h_to(dn, me, b, CHUNKS + b, hid.at[piece(b), :])
    for k in range(CHUNKS):
        h_to(sib, me, k, 2 * CHUNKS + k, hid.at[piece(k), :])
    sem = 3 * CHUNKS
    for a, b in zip(low, high):
        h_wait(dn, a)
        h_to(up, dn, a, sem, None)
        h_to(sib, dn, a, sem + 1, None)
        h_wait(up, b)
        h_to(dn, up, b, sem + 2, None)
        h_to(sib, up, b, sem + 3, None)
        sem += 4
    for k in low:
        h_wait(dn_chip * 2 + 1 - core, k)

    for other in range(1, N_CTX):
        dev = lax.rem(me + other, N_CTX)
        go(send(docs, dall.at[me], d_send.at[other], d_recv.at[me], dev))
    dall[me] = docs[...]

    for i, (far_chip, far) in enumerate(((up_chip, up), (dn_chip, dn), (opp_chip, opp))):
        for j in range(2):
            dev = far_chip * 2 + j
            feats = pl.ds(pl.multiple_of(dev * HDIM, HDIM), HDIM)
            go(send(qry.at[:, feats], qall.at[me], q_send.at[2 * i + j], q_recv.at[me], dev))
            go(send(cot.at[:, feats], call.at[me], c_send.at[2 * i + j], c_recv.at[me], dev))
        feats = pl.ds(pl.multiple_of(far_chip * HDIM, HDIM), HDIM)
        go(send(val.at[:, feats], vall.at[me], v_send.at[i], v_recv.at[me], far))
    sib_feats = pl.ds(pl.multiple_of(sib * HDIM, HDIM), HDIM)
    go(send(qry.at[:, sib_feats], qall.at[me], q_send.at[6], q_recv.at[me], sib))
    go(send(cot.at[:, sib_feats], call.at[me], c_send.at[6], c_recv.at[me], sib))
    go(send(val.at[:, kv_head], vall.at[me], v_send.at[3], v_recv.at[me], sib))

    for copy in local_copies:
        copy.wait()

    def project(p):
        block = hall[pl.ds(2 * p, 2)].reshape(2 * ROWS, hall.shape[2])
        out = jnp.dot(block, wown[...], preferred_element_type=jnp.float32)
        rows = pl.ds(pl.multiple_of(p * 2 * ROWS, 2 * ROWS), 2 * ROWS)
        kbuf[rows, own_half] = out.astype(jnp.bfloat16)
        go(send(kbuf.at[rows, own_half], kbuf.at[rows, own_half], k_send.at[p], k_recv.at[p], sib))

    for k in range(CHUNKS):
        h_wait(sib, k)
    project(chip)

    for a, b in zip(high, low):
        h_wait(dn, a)
        h_to(sib, dn, a, sem, None)
        h_wait(up, b)
        h_to(sib, up, b, sem + 1, None)
        sem += 2
    for k in range(CHUNKS):
        h_wait(up_chip * 2 + 1 - core, k)
    project(up_chip)
    for k in high:
        h_wait(dn_chip * 2 + 1 - core, k)
    project(dn_chip)
    for a, b in zip(low, high):
        h_wait(opp, a)
        h_to(sib, opp, a, sem, None)
        h_wait(opp, b)
        h_to(sib, opp, b, sem + 1, None)
        sem += 2
    for k in range(CHUNKS):
        h_wait(opp_chip * 2 + 1 - core, k)
    project(opp_chip)

    for i, far in enumerate((up, dn, opp)):
        send(vall.at[far], vall.at[far], v_send.at[0], v_recv.at[far], sib).wait_recv()
        go(send(vall.at[far], vall.at[far], v_send.at[4 + i], v_recv.at[far], sib))
    for other in range(1, N_CTX):
        src = lax.rem(me + other, N_CTX)
        send(qall.at[src], qall.at[src], q_send.at[0], q_recv.at[src], sib).wait_recv()
        send(call.at[src], call.at[src], c_send.at[0], c_recv.at[src], sib).wait_recv()
        send(docs, dall.at[src], d_send.at[0], d_recv.at[src], sib).wait_recv()
    for p in (chip, up_chip, dn_chip, opp_chip):
        src = 2 * p + 1 - core
        send(vall.at[src], vall.at[src], v_send.at[0], v_recv.at[src], sib).wait_recv()
        rows = pl.ds(pl.multiple_of(p * 2 * ROWS, 2 * ROWS), 2 * ROWS)
        half = kbuf.at[rows, sib_half]
        send(half, half, k_send.at[0], k_recv.at[p], sib).wait_recv()

    doc_rows = [dall[s] for s in range(N_CTX)]
    starts = [jnp.zeros(row.shape, jnp.float32) for row in doc_rows]
    for v in range(3):
        total = jnp.zeros((1, 1), jnp.float32)
        for row in doc_rows:
            total = total + jnp.sum(jnp.where(row == v, 1.0, 0.0), axis=1, keepdims=True)
        starts = [s + jnp.where(row > v, total, 0.0) for s, row in zip(starts, doc_rows)]

    dkacc[...] = jnp.zeros_like(dkacc)
    block = 2 * ROWS
    for p in range(CHIPS):
        first = max(p - 2, 0)
        keys = (p + 1 - first) * block
        rows = pl.ds(first * block, keys)
        q = qall[2 * p : 2 * p + 2].reshape(block, HDIM)
        c = call[2 * p : 2 * p + 2].reshape(block, HDIM)
        v = vall[2 * first : 2 * p + 2].reshape(keys, HDIM)
        start = jnp.concatenate([starts[2 * p], starts[2 * p + 1]], axis=1).astype(jnp.int32)
        t = jnp.tanh(nt(kbuf[rows, :], q) * (1.0 / (HDIM**0.5 * softcap)))
        key_pos = first * block + lax.broadcasted_iota(jnp.int32, (keys, block), 0)
        query_pos = p * block + lax.broadcasted_iota(jnp.int32, (keys, block), 1)
        allowed = (key_pos <= query_pos) & (key_pos >= start)
        e = jnp.where(allowed, jnp.exp(softcap * t), 0.0)
        prob_grad = nt(v, c)
        norm = 1.0 / jnp.sum(e, axis=0, keepdims=True)
        row_dot = jnp.sum(e * prob_grad, axis=0, keepdims=True) * norm
        score_grad = (e * norm) * (prob_grad - row_dot) * (1.0 - t * t)
        dkacc[rows, :] += jnp.dot(
            score_grad.astype(jnp.bfloat16), q, preferred_element_type=jnp.float32
        )

    scale = 1.0 / HDIM**0.5
    dksend[...] = (dkacc[:, sib_half] * scale).astype(jnp.bfloat16)
    swap = send(dksend, dkrecv, g_send.at[0], g_recv.at[0], sib)
    go(swap)
    swap.wait_recv()
    dk = dkacc[:, own_half] * scale + dkrecv[...].astype(jnp.float32)
    dkown[...] = dk.T.astype(jnp.bfloat16)

    width = 512

    @pl.loop(0, grad.shape[0] // width)
    def _(i):
        cols = pl.ds(pl.multiple_of(i * width, width), width)
        h = hall[:, :, cols].reshape(N_CTX * ROWS, width)
        g = jnp.dot(dkown[...], h, preferred_element_type=jnp.float32).T
        grad[cols, :] = g.astype(jnp.bfloat16)
        stepped[cols, :] = (wown[cols, :].astype(jnp.float32) - step_size * g).astype(jnp.bfloat16)

    for copy in started:
        copy.wait_send()


def local_gradient(hidden, queries, values, cotangent, key_weight, doc_ids, round_index):
    depth = hidden.shape[1]
    dma = pltpu.SemaphoreType.DMA
    bf16, f32 = jnp.bfloat16, jnp.float32
    hbm = pl.BlockSpec(memory_space=pltpu.HBM)
    smem = pl.BlockSpec(memory_space=pltpu.SMEM)
    vmem = pl.BlockSpec(memory_space=pltpu.VMEM)
    seq = N_CTX * ROWS
    return pl.pallas_call(
        gradient_kernel,
        out_shape=[jax.ShapeDtypeStruct((depth, 128), bf16)] * 2
        + [jax.ShapeDtypeStruct((1,), jnp.int32)],
        in_specs=[hbm] * 5 + [vmem, smem],
        out_specs=[vmem, vmem, smem],
        scratch_shapes=[
            pltpu.VMEM((N_CTX, ROWS, depth), bf16),
            pltpu.VMEM((N_CTX, ROWS, HDIM), bf16),
            pltpu.VMEM((N_CTX, ROWS, HDIM), bf16),
            pltpu.VMEM((N_CTX, ROWS, HDIM), bf16),
            pltpu.VMEM((N_CTX, 1, ROWS), jnp.int32),
            pltpu.VMEM((depth, 128), bf16),
            pltpu.VMEM((seq, HDIM), bf16),
            pltpu.VMEM((seq, HDIM), f32),
            pltpu.VMEM((seq, 128), bf16),
            pltpu.VMEM((seq, 128), bf16),
            pltpu.VMEM((128, seq), bf16),
            dma((5,)),
            dma((N_CTX, CHUNKS)),
            dma((7 * CHUNKS,)),
            dma((N_CTX,)),
            dma((7,)),
            dma((N_CTX,)),
            dma((7,)),
            dma((N_CTX,)),
            dma((7,)),
            dma((N_CTX,)),
            dma((N_CTX,)),
            dma((CHIPS,)),
            dma((CHIPS,)),
            dma((1,)),
            dma((1,)),
        ],
        compiler_params=pltpu.CompilerParams(
            collective_id=0, has_side_effects=True, vmem_limit_bytes=60 * 1024 * 1024
        ),
        name="gradient",
    )(hidden, queries, values, cotangent, key_weight, doc_ids, round_index)


def on_device(hidden, queries, values, cotangent, key_weight, doc_ids, round_index):
    gradient, stepped, mask = local_gradient(
        hidden[0], queries[0], values[0], cotangent[0], key_weight[0], doc_ids, round_index
    )
    averaged = gossip_rounds(stepped, mask[0])
    return (averaged[None], gradient[None])


def solution(mesh):
    return jax.shard_map(
        on_device,
        mesh=mesh,
        in_specs=(
            P("rep", "ctx", None),
            P("rep", "ctx", None),
            P("rep", "ctx", None),
            P("rep", "ctx", None),
            P("rep", None, "ctx"),
            P("rep", "ctx"),
            P(),
        ),
        out_specs=(P("rep", None, "ctx"), P("rep", None, "ctx")),
        check_vma=False,
    )
```

```python
from functools import partial

import jax
import jax.numpy as jnp
from jax import lax
from jax.experimental import pallas as pl
from jax.experimental.pallas import tpu as pltpu
from jax.sharding import PartitionSpec as P

MESH = pl.DeviceIdType.MESH

HDIM = 256
HEADS = 8
KVH = 4
GOSSIP = 3
N_CTX = 8
CHIPS = 4
ROWS = 128
CHUNKS = 4
RANKS = 6

softcap = 50.0
step_size = 0.0005


PIECES = 7
INNER = 3


def gossip_plan(bits):
    outer = tuple(bit for bit in bits if bit < INNER)
    inner = tuple(bit for bit in bits if bit >= INNER)
    if not (outer and inner):
        outer, inner = (), bits
    depth = 1 if outer else 0
    if len(inner) == 1:
        plan = [("swap", inner, depth)]
    else:
        plan = [("scatter", inner, depth), ("gather", inner, depth)]
    if outer:
        plan = [("scatter", outer, 0)] + plan + [("gather", outer, 0)]
    return plan


def gossip_kernel(bits, x, out, acc, landing, send_sem, recv_sem):
    me = lax.axis_index("rep")
    plan = gossip_plan(bits)
    stages = len(plan)
    reduced = max(s for s, (kind, _, _) in enumerate(plan) if kind != "gather")
    rows = x.shape[0] // PIECES
    digit = {bit: lax.rem(me // (1 << bit), 2) for bit in bits}

    def peers(group):
        place = sum(digit[bit] << i for i, bit in enumerate(group))
        others = []
        for flip in range(1, 1 << len(group)):
            device, there = me, 0
            for i, bit in enumerate(group):
                if flip >> i & 1:
                    device = device + (1 - 2 * digit[bit]) * (1 << bit)
                    there = there + ((1 - digit[bit]) << i)
                else:
                    there = there + (digit[bit] << i)
            others.append((device, there))
        return place, others

    groups = {group: peers(group) for _, group, _ in plan}
    met = [device for _, others in groups.values() for device, _ in others]
    barrier = pltpu.get_barrier_semaphore()
    for device in met:
        pl.semaphore_signal(barrier, inc=1, device_id={"rep": device}, device_id_type=MESH)
    pl.semaphore_wait(barrier, len(met))

    def region(piece, depth):
        base, size = piece * rows, rows
        if depth:
            group = plan[0][1]
            size //= 1 << len(group)
            base = base + groups[group][0] * size
        return base, size

    def at(ref, base, size):
        return ref.at[pl.ds(pl.multiple_of(base, 16), size), :]

    def landed(stage, slot, piece, size):
        return landing.at[stage, slot, pl.ds(pl.multiple_of(piece * size, 16), size), :]

    def transfers(piece, stage, arriving=False):
        kind, group, depth = plan[stage]
        base, size = region(piece, depth)
        src = x if stage == 0 else acc
        place, others = groups[group]
        part = size if kind == "swap" else size >> len(group)
        for slot, (device, there) in enumerate(others):
            if kind == "gather":
                sent = at(out, base + place * part, part)
                dst = at(out, base + there * part, part) if arriving else sent
            else:
                sent = at(src, base if kind == "swap" else base + there * part, part)
                dst = landed(stage, slot, piece, part)
            yield pltpu.make_async_remote_copy(
                src_ref=sent, dst_ref=dst, send_sem=send_sem.at[piece, stage, slot],
                recv_sem=recv_sem.at[piece, stage, slot], device_id={"rep": device},
                device_id_type=MESH,
            )

    def start(piece, stage):
        for copy in transfers(piece, stage):
            copy.start()

    def finish(piece, stage):
        for copy in transfers(piece, stage, arriving=True):
            copy.wait_recv()
        kind, group, depth = plan[stage]
        if kind != "gather":
            base, size = region(piece, depth)
            place, others = groups[group]
            if kind == "scatter":
                size >>= len(group)
                base = base + place * size
            total = at(x if stage == 0 else acc, base, size)[...].astype(jnp.float32)
            for slot in range(len(others)):
                total = total + landed(stage, slot, piece, size)[...].astype(jnp.float32)
            mean = total * (1.0 / (1 << len(group)))
            at(out if stage == reduced else acc, base, size)[...] = mean.astype(jnp.bfloat16)

    @pl.loop(0, PIECES)
    def _(piece):
        start(piece, 0)

    for stage in range(stages):

        @pl.loop(0, PIECES)
        def _(piece, stage=stage):
            finish(piece, stage)
            if stage + 1 < stages:
                start(piece, stage + 1)

    @pl.loop(0, PIECES)
    def _(piece):
        for stage in range(stages):
            for copy in transfers(piece, stage):
                copy.wait_send()


def gossip(bits, number):
    def run(stepped):
        shape = stepped.shape
        plan = gossip_plan(bits)
        sums = [s for s, (kind, _, _) in enumerate(plan) if kind != "gather"]
        slots = max((1 << len(group)) - 1 for _, group, _ in plan)
        deepest = max(shape[0] >> (0 if kind == "swap" else len(group)) for kind, group, _ in plan)
        vmem = pl.BlockSpec(memory_space=pltpu.VMEM)
        return pl.pallas_call(
            partial(gossip_kernel, bits),
            out_shape=jax.ShapeDtypeStruct(shape, jnp.bfloat16),
            in_specs=[vmem],
            out_specs=vmem,
            scratch_shapes=[
                pltpu.VMEM(shape, jnp.bfloat16),
                pltpu.VMEM((max(sums) + 1, slots, deepest, shape[1]), jnp.bfloat16),
            ]
            + [pltpu.SemaphoreType.DMA((PIECES, len(plan), slots))] * 2,
            compiler_params=pltpu.CompilerParams(
                collective_id=number, has_side_effects=True, vmem_limit_bytes=24 * 1024 * 1024
            ),
            name="gossip",
        )(stepped)

    return run


def gossip_rounds(stepped, mask):
    branches = []
    for case in range(1 << RANKS):
        bits = tuple(bit for bit in range(RANKS) if case >> bit & 1)
        if 1 <= len(bits) <= GOSSIP:
            branches.append(gossip(bits, 1 + case))
        else:
            branches.append(lambda kept: kept)
    return lax.switch(mask, branches, stepped)


def nt(a, b):
    return lax.dot_general(a, b, (((1,), (1,)), ((), ())), preferred_element_type=jnp.float32)


def gradient_kernel(
    hid, qry, val, cot, wgt, docs, rounds, grad, stepped, mask,
    hall, qall, call, vall, dall, wown, kbuf, dkacc, dksend, dkrecv, dkown,
    local, h_recv, h_send, q_recv, q_send, c_recv, c_send, v_recv, v_send, d_recv, d_send,
    k_recv, k_send, g_recv, g_send,
):
    me = lax.axis_index("ctx")
    chip = me // 2
    core = lax.rem(me, 2)
    sib = chip * 2 + (1 - core)
    up_chip = lax.rem(chip + 1, CHIPS)
    dn_chip = lax.rem(chip + 3, CHIPS)
    opp_chip = lax.rem(chip + 2, CHIPS)
    up = up_chip * 2 + core
    dn = dn_chip * 2 + core
    opp = opp_chip * 2 + core
    rows_of = ROWS // CHUNKS

    def send(src, dst, ssem, rsem, dev):
        return pltpu.make_async_remote_copy(
            src_ref=src, dst_ref=dst, send_sem=ssem, recv_sem=rsem,
            device_id={"ctx": dev}, device_id_type=MESH,
        )

    mask[0] = (1 << rounds[0]) | (1 << rounds[1]) | (1 << rounds[2])
    barrier = pltpu.get_barrier_semaphore()
    for other in (sib, up, dn):
        pl.semaphore_signal(barrier, inc=1, device_id={"ctx": other}, device_id_type=MESH)

    head = pl.ds(pl.multiple_of(me * HDIM, HDIM), HDIM)
    kv_head = pl.ds(pl.multiple_of(chip * HDIM, HDIM), HDIM)
    own_half = pl.ds(pl.multiple_of(core * 128, 128), 128)
    sib_half = pl.ds(pl.multiple_of((1 - core) * 128, 128), 128)
    local_copies = [
        pltpu.make_async_copy(hid, hall.at[me], local.at[0]),
        pltpu.make_async_copy(wgt, wown, local.at[1]),
        pltpu.make_async_copy(qry.at[:, head], qall.at[me], local.at[2]),
        pltpu.make_async_copy(cot.at[:, head], call.at[me], local.at[3]),
        pltpu.make_async_copy(val.at[:, kv_head], vall.at[me], local.at[4]),
    ]
    for copy in local_copies:
        copy.start()
    pl.semaphore_wait(barrier, 3)

    started = []

    def go(copy):
        copy.start()
        started.append(copy)

    def piece(k):
        return pl.ds(k * rows_of, rows_of)

    low = list(range(CHUNKS // 2))
    high = list(range(CHUNKS // 2, CHUNKS))

    def h_to(dev, origin, k, sem, src=None):
        slot = hall.at[origin, piece(k), :]
        go(send(slot if src is None else src, slot, h_send.at[sem], h_recv.at[origin, k], dev))

    def h_wait(origin, k):
        slot = hall.at[origin, piece(k), :]
        send(slot, slot, h_send.at[0], h_recv.at[origin, k], sib).wait_recv()

    for a, b in zip(low + high, high + low):
        h_to(up, me, a, a, hid.at[piece(a), :])
        h_to(dn, me, b, CHUNKS + b, hid.at[piece(b), :])
    for k in range(CHUNKS):
        h_to(sib, me, k, 2 * CHUNKS + k, hid.at[piece(k), :])
    sem = 3 * CHUNKS
    for a, b in zip(low, high):
        h_wait(dn, a)
        h_to(up, dn, a, sem, None)
        h_to(sib, dn, a, sem + 1, None)
        h_wait(up, b)
        h_to(dn, up, b, sem + 2, None)
        h_to(sib, up, b, sem + 3, None)
        sem += 4
    for k in low:
        h_wait(dn_chip * 2 + 1 - core, k)

    for other in range(1, N_CTX):
        dev = lax.rem(me + other, N_CTX)
        go(send(docs, dall.at[me], d_send.at[other], d_recv.at[me], dev))
    dall[me] = docs[...]

    for i, (far_chip, far) in enumerate(((up_chip, up), (dn_chip, dn), (opp_chip, opp))):
        for j in range(2):
            dev = far_chip * 2 + j
            feats = pl.ds(pl.multiple_of(dev * HDIM, HDIM), HDIM)
            go(send(qry.at[:, feats], qall.at[me], q_send.at[2 * i + j], q_recv.at[me], dev))
            go(send(cot.at[:, feats], call.at[me], c_send.at[2 * i + j], c_recv.at[me], dev))
        feats = pl.ds(pl.multiple_of(far_chip * HDIM, HDIM), HDIM)
        go(send(val.at[:, feats], vall.at[me], v_send.at[i], v_recv.at[me], far))
    sib_feats = pl.ds(pl.multiple_of(sib * HDIM, HDIM), HDIM)
    go(send(qry.at[:, sib_feats], qall.at[me], q_send.at[6], q_recv.at[me], sib))
    go(send(cot.at[:, sib_feats], call.at[me], c_send.at[6], c_recv.at[me], sib))
    go(send(val.at[:, kv_head], vall.at[me], v_send.at[3], v_recv.at[me], sib))

    for copy in local_copies:
        copy.wait()

    def project(p):
        block = hall[pl.ds(2 * p, 2)].reshape(2 * ROWS, hall.shape[2])
        out = jnp.dot(block, wown[...], preferred_element_type=jnp.float32)
        rows = pl.ds(pl.multiple_of(p * 2 * ROWS, 2 * ROWS), 2 * ROWS)
        kbuf[rows, own_half] = out.astype(jnp.bfloat16)
        go(send(kbuf.at[rows, own_half], kbuf.at[rows, own_half], k_send.at[p], k_recv.at[p], sib))

    for k in range(CHUNKS):
        h_wait(sib, k)
    project(chip)

    for a, b in zip(high, low):
        h_wait(dn, a)
        h_to(sib, dn, a, sem, None)
        h_wait(up, b)
        h_to(sib, up, b, sem + 1, None)
        sem += 2
    for k in range(CHUNKS):
        h_wait(up_chip * 2 + 1 - core, k)
    project(up_chip)
    for k in high:
        h_wait(dn_chip * 2 + 1 - core, k)
    project(dn_chip)
    for a, b in zip(low, high):
        h_wait(opp, a)
        h_to(sib, opp, a, sem, None)
        h_wait(opp, b)
        h_to(sib, opp, b, sem + 1, None)
        sem += 2
    for k in range(CHUNKS):
        h_wait(opp_chip * 2 + 1 - core, k)
    project(opp_chip)

    for i, far in enumerate((up, dn, opp)):
        send(vall.at[far], vall.at[far], v_send.at[0], v_recv.at[far], sib).wait_recv()
        go(send(vall.at[far], vall.at[far], v_send.at[4 + i], v_recv.at[far], sib))
    for other in range(1, N_CTX):
        src = lax.rem(me + other, N_CTX)
        send(qall.at[src], qall.at[src], q_send.at[0], q_recv.at[src], sib).wait_recv()
        send(call.at[src], call.at[src], c_send.at[0], c_recv.at[src], sib).wait_recv()
        send(docs, dall.at[src], d_send.at[0], d_recv.at[src], sib).wait_recv()
    for p in (chip, up_chip, dn_chip, opp_chip):
        src = 2 * p + 1 - core
        send(vall.at[src], vall.at[src], v_send.at[0], v_recv.at[src], sib).wait_recv()
        rows = pl.ds(pl.multiple_of(p * 2 * ROWS, 2 * ROWS), 2 * ROWS)
        half = kbuf.at[rows, sib_half]
        send(half, half, k_send.at[0], k_recv.at[p], sib).wait_recv()

    doc_rows = [dall[s] for s in range(N_CTX)]
    starts = [jnp.zeros(row.shape, jnp.float32) for row in doc_rows]
    for v in range(3):
        total = jnp.zeros((1, 1), jnp.float32)
        for row in doc_rows:
            total = total + jnp.sum(jnp.where(row == v, 1.0, 0.0), axis=1, keepdims=True)
        starts = [s + jnp.where(row > v, total, 0.0) for s, row in zip(starts, doc_rows)]

    dkacc[...] = jnp.zeros_like(dkacc)
    block = 2 * ROWS
    for p in range(CHIPS):
        first = max(p - 2, 0)
        keys = (p + 1 - first) * block
        rows = pl.ds(first * block, keys)
        q = qall[2 * p : 2 * p + 2].reshape(block, HDIM)
        c = call[2 * p : 2 * p + 2].reshape(block, HDIM)
        v = vall[2 * first : 2 * p + 2].reshape(keys, HDIM)
        start = jnp.concatenate([starts[2 * p], starts[2 * p + 1]], axis=1).astype(jnp.int32)
        t = jnp.tanh(nt(kbuf[rows, :], q) * (1.0 / (HDIM**0.5 * softcap)))
        key_pos = first * block + lax.broadcasted_iota(jnp.int32, (keys, block), 0)
        query_pos = p * block + lax.broadcasted_iota(jnp.int32, (keys, block), 1)
        allowed = (key_pos <= query_pos) & (key_pos >= start)
        e = jnp.where(allowed, jnp.exp(softcap * t), 0.0)
        prob_grad = nt(v, c)
        norm = 1.0 / jnp.sum(e, axis=0, keepdims=True)
        row_dot = jnp.sum(e * prob_grad, axis=0, keepdims=True) * norm
        score_grad = (e * norm) * (prob_grad - row_dot) * (1.0 - t * t)
        dkacc[rows, :] += jnp.dot(
            score_grad.astype(jnp.bfloat16), q, preferred_element_type=jnp.float32
        )

    scale = 1.0 / HDIM**0.5
    dksend[...] = (dkacc[:, sib_half] * scale).astype(jnp.bfloat16)
    swap = send(dksend, dkrecv, g_send.at[0], g_recv.at[0], sib)
    go(swap)
    swap.wait_recv()
    dk = dkacc[:, own_half] * scale + dkrecv[...].astype(jnp.float32)
    dkown[...] = dk.T.astype(jnp.bfloat16)

    width = 512

    @pl.loop(0, grad.shape[0] // width)
    def _(i):
        cols = pl.ds(pl.multiple_of(i * width, width), width)
        h = hall[:, :, cols].reshape(N_CTX * ROWS, width)
        g = jnp.dot(dkown[...], h, preferred_element_type=jnp.float32).T
        grad[cols, :] = g.astype(jnp.bfloat16)
        stepped[cols, :] = (wown[cols, :].astype(jnp.float32) - step_size * g).astype(jnp.bfloat16)

    for copy in started:
        copy.wait_send()


def local_gradient(hidden, queries, values, cotangent, key_weight, doc_ids, round_index):
    depth = hidden.shape[1]
    dma = pltpu.SemaphoreType.DMA
    bf16, f32 = jnp.bfloat16, jnp.float32
    hbm = pl.BlockSpec(memory_space=pltpu.HBM)
    smem = pl.BlockSpec(memory_space=pltpu.SMEM)
    vmem = pl.BlockSpec(memory_space=pltpu.VMEM)
    seq = N_CTX * ROWS
    return pl.pallas_call(
        gradient_kernel,
        out_shape=[jax.ShapeDtypeStruct((depth, 128), bf16)] * 2
        + [jax.ShapeDtypeStruct((1,), jnp.int32)],
        in_specs=[hbm] * 5 + [vmem, smem],
        out_specs=[vmem, vmem, smem],
        scratch_shapes=[
            pltpu.VMEM((N_CTX, ROWS, depth), bf16),
            pltpu.VMEM((N_CTX, ROWS, HDIM), bf16),
            pltpu.VMEM((N_CTX, ROWS, HDIM), bf16),
            pltpu.VMEM((N_CTX, ROWS, HDIM), bf16),
            pltpu.VMEM((N_CTX, 1, ROWS), jnp.int32),
            pltpu.VMEM((depth, 128), bf16),
            pltpu.VMEM((seq, HDIM), bf16),
            pltpu.VMEM((seq, HDIM), f32),
            pltpu.VMEM((seq, 128), bf16),
            pltpu.VMEM((seq, 128), bf16),
            pltpu.VMEM((128, seq), bf16),
            dma((5,)),
            dma((N_CTX, CHUNKS)),
            dma((7 * CHUNKS,)),
            dma((N_CTX,)),
            dma((7,)),
            dma((N_CTX,)),
            dma((7,)),
            dma((N_CTX,)),
            dma((7,)),
            dma((N_CTX,)),
            dma((N_CTX,)),
            dma((CHIPS,)),
            dma((CHIPS,)),
            dma((1,)),
            dma((1,)),
        ],
        compiler_params=pltpu.CompilerParams(
            collective_id=0, has_side_effects=True, vmem_limit_bytes=60 * 1024 * 1024
        ),
        name="gradient",
    )(hidden, queries, values, cotangent, key_weight, doc_ids, round_index)


def on_device(hidden, queries, values, cotangent, key_weight, doc_ids, round_index):
    gradient, stepped, mask = local_gradient(
        hidden[0], queries[0], values[0], cotangent[0], key_weight[0], doc_ids, round_index
    )
    averaged = gossip_rounds(stepped, mask[0])
    return (averaged[None], gradient[None])


def solution(mesh):
    return jax.shard_map(
        on_device,
        mesh=mesh,
        in_specs=(
            P("rep", "ctx", None),
            P("rep", "ctx", None),
            P("rep", "ctx", None),
            P("rep", "ctx", None),
            P("rep", None, "ctx"),
            P("rep", "ctx"),
            P(),
        ),
        out_specs=(P("rep", None, "ctx"), P("rep", None, "ctx")),
        check_vma=False,
    )
```

```python
import itertools
from functools import partial

import jax
import jax.numpy as jnp
from jax import lax
from jax.experimental import pallas as pl
from jax.experimental.pallas import tpu as pltpu
from jax.sharding import PartitionSpec as P

MESH = pl.DeviceIdType.MESH

HDIM = 256
HEADS = 8
KVH = 4
GOSSIP = 3
N_CTX = 8
CHIPS = 4
ROWS = 128
CHUNKS = 4
AHEAD = 2
RANKS = 6

softcap = 50.0
step_size = 0.0005


PIECES = 7
INNER = 3


def gossip_plan(bits):
    outer = tuple(bit for bit in bits if bit < INNER)
    inner = tuple(bit for bit in bits if bit >= INNER)
    if not (outer and inner):
        outer, inner = (), bits
    depth = 1 if outer else 0
    if len(inner) == 1:
        plan = [("swap", inner, depth)]
    else:
        plan = [("scatter", inner, depth), ("gather", inner, depth)]
    if outer:
        plan = [("scatter", outer, 0)] + plan + [("gather", outer, 0)]
    return plan


def gossip_kernel(bits, x, out, acc, landing, send_sem, recv_sem):
    me = lax.axis_index("rep")
    plan = gossip_plan(bits)
    stages = len(plan)
    reduced = max(s for s, (kind, _, _) in enumerate(plan) if kind != "gather")
    rows = x.shape[0] // PIECES
    digit = {bit: lax.rem(me // (1 << bit), 2) for bit in bits}

    def peers(group):
        place = sum(digit[bit] << i for i, bit in enumerate(group))
        others = []
        for flip in range(1, 1 << len(group)):
            device, there = me, 0
            for i, bit in enumerate(group):
                if flip >> i & 1:
                    device = device + (1 - 2 * digit[bit]) * (1 << bit)
                    there = there + ((1 - digit[bit]) << i)
                else:
                    there = there + (digit[bit] << i)
            others.append((device, there))
        return place, others

    groups = {group: peers(group) for _, group, _ in plan}
    met = [device for _, others in groups.values() for device, _ in others]
    barrier = pltpu.get_barrier_semaphore()
    for device in met:
        pl.semaphore_signal(barrier, inc=1, device_id={"rep": device}, device_id_type=MESH)
    pl.semaphore_wait(barrier, len(met))

    def region(piece, depth):
        base, size = piece * rows, rows
        if depth:
            group = plan[0][1]
            size //= 1 << len(group)
            base = base + groups[group][0] * size
        return base, size

    def at(ref, base, size):
        return ref.at[pl.ds(pl.multiple_of(base, 16), size), :]

    def landed(stage, slot, piece, size):
        return landing.at[stage, slot, pl.ds(pl.multiple_of(piece * size, 16), size), :]

    def transfers(piece, stage, arriving=False):
        kind, group, depth = plan[stage]
        base, size = region(piece, depth)
        src = x if stage == 0 else acc
        place, others = groups[group]
        part = size if kind == "swap" else size >> len(group)
        for slot, (device, there) in enumerate(others):
            if kind == "gather":
                sent = at(out, base + place * part, part)
                dst = at(out, base + there * part, part) if arriving else sent
            else:
                sent = at(src, base if kind == "swap" else base + there * part, part)
                dst = landed(stage, slot, piece, part)
            yield pltpu.make_async_remote_copy(
                src_ref=sent, dst_ref=dst, send_sem=send_sem.at[piece, stage, slot],
                recv_sem=recv_sem.at[piece, stage, slot], device_id={"rep": device},
                device_id_type=MESH,
            )

    def start(piece, stage):
        for copy in transfers(piece, stage):
            copy.start()

    def finish(piece, stage):
        for copy in transfers(piece, stage, arriving=True):
            copy.wait_recv()
        kind, group, depth = plan[stage]
        if kind != "gather":
            base, size = region(piece, depth)
            place, others = groups[group]
            if kind == "scatter":
                size >>= len(group)
                base = base + place * size
            total = at(x if stage == 0 else acc, base, size)[...].astype(jnp.float32)
            for slot in range(len(others)):
                total = total + landed(stage, slot, piece, size)[...].astype(jnp.float32)
            mean = total * (1.0 / (1 << len(group)))
            at(out if stage == reduced else acc, base, size)[...] = mean.astype(jnp.bfloat16)

    @pl.loop(0, PIECES)
    def _(piece):
        start(piece, 0)

    for stage in range(stages):

        @pl.loop(0, PIECES)
        def _(piece, stage=stage):
            finish(piece, stage)
            if stage + 1 < stages:
                start(piece, stage + 1)

    @pl.loop(0, PIECES)
    def _(piece):
        for stage in range(stages):
            for copy in transfers(piece, stage):
                copy.wait_send()


def gossip(bits, number):
    def run(stepped):
        shape = stepped.shape
        plan = gossip_plan(bits)
        sums = [s for s, (kind, _, _) in enumerate(plan) if kind != "gather"]
        slots = max((1 << len(group)) - 1 for _, group, _ in plan)
        deepest = max(shape[0] >> (0 if kind == "swap" else len(group)) for kind, group, _ in plan)
        vmem = pl.BlockSpec(memory_space=pltpu.VMEM)
        return pl.pallas_call(
            partial(gossip_kernel, bits),
            out_shape=jax.ShapeDtypeStruct(shape, jnp.bfloat16),
            in_specs=[vmem],
            out_specs=vmem,
            scratch_shapes=[
                pltpu.VMEM(shape, jnp.bfloat16),
                pltpu.VMEM((max(sums) + 1, slots, deepest, shape[1]), jnp.bfloat16),
            ]
            + [pltpu.SemaphoreType.DMA((PIECES, len(plan), slots))] * 2,
            compiler_params=pltpu.CompilerParams(
                collective_id=number, has_side_effects=True, vmem_limit_bytes=24 * 1024 * 1024
            ),
            name="gossip",
        )(stepped)

    return run


def gossip_rounds(stepped, mask):
    branches = []
    for case in range(1 << RANKS):
        bits = tuple(bit for bit in range(RANKS) if case >> bit & 1)
        if 1 <= len(bits) <= GOSSIP:
            branches.append(gossip(bits, 1 + case))
        else:
            branches.append(lambda kept: kept)
    return lax.switch(mask, branches, stepped)


def nt(a, b):
    return lax.dot_general(a, b, (((1,), (1,)), ((), ())), preferred_element_type=jnp.float32)


def gradient_kernel(
    hid, qry, val, cot, wgt, docs, rounds, grad, stepped, mask,
    hall, qall, call, vall, dall, wown, kbuf, dkacc, dksend, dkrecv, dkown, first_pos,
    local, h_recv, h_send, q_recv, q_send, c_recv, c_send, v_recv, v_send, d_recv, d_send,
    k_recv, k_send, g_recv, g_send,
):
    me = lax.axis_index("ctx")
    chip = me // 2
    core = lax.rem(me, 2)
    sib = chip * 2 + (1 - core)
    way = 1 - 2 * lax.rem(lax.axis_index("rep"), 2)
    up_chip = lax.rem(chip + CHIPS + way, CHIPS)
    dn_chip = lax.rem(chip + CHIPS - way, CHIPS)
    opp_chip = lax.rem(chip + 2, CHIPS)
    up = up_chip * 2 + core
    dn = dn_chip * 2 + core
    opp = opp_chip * 2 + core
    rows_of = ROWS // CHUNKS

    def send(src, dst, ssem, rsem, dev):
        return pltpu.make_async_remote_copy(
            src_ref=src, dst_ref=dst, send_sem=ssem, recv_sem=rsem,
            device_id={"ctx": dev}, device_id_type=MESH,
        )

    mask[0] = (1 << rounds[0]) | (1 << rounds[1]) | (1 << rounds[2])
    barrier = pltpu.get_barrier_semaphore()
    for other in (sib, up, dn):
        pl.semaphore_signal(barrier, inc=1, device_id={"ctx": other}, device_id_type=MESH)

    head = pl.ds(pl.multiple_of(me * HDIM, HDIM), HDIM)
    kv_head = pl.ds(pl.multiple_of(chip * HDIM, HDIM), HDIM)
    own_half = pl.ds(pl.multiple_of(core * 128, 128), 128)
    sib_half = pl.ds(pl.multiple_of((1 - core) * 128, 128), 128)
    local_copies = [
        pltpu.make_async_copy(hid, hall.at[me], local.at[0]),
        pltpu.make_async_copy(wgt, wown, local.at[1]),
        pltpu.make_async_copy(qry.at[:, head], qall.at[me], local.at[2]),
        pltpu.make_async_copy(cot.at[:, head], call.at[me], local.at[3]),
        pltpu.make_async_copy(val.at[:, kv_head], vall.at[me], local.at[4]),
    ]
    for copy in local_copies:
        copy.start()
    pl.semaphore_wait(barrier, 3)

    started = []

    def go(copy):
        copy.start()
        started.append(copy)

    def piece(k):
        return pl.ds(k * rows_of, rows_of)

    low = list(range(AHEAD))
    high = list(range(AHEAD, CHUNKS))

    def h_to(dev, origin, k, sem, src=None):
        slot = hall.at[origin, piece(k), :]
        go(send(slot if src is None else src, slot, h_send.at[sem], h_recv.at[origin, k], dev))

    def h_wait(origin, k):
        slot = hall.at[origin, piece(k), :]
        send(slot, slot, h_send.at[0], h_recv.at[origin, k], sib).wait_recv()

    for a, b in zip(low + high, high + low):
        h_to(up, me, a, a, hid.at[piece(a), :])
        h_to(dn, me, b, CHUNKS + b, hid.at[piece(b), :])
    for k in range(CHUNKS):
        h_to(sib, me, k, 2 * CHUNKS + k, hid.at[piece(k), :])
    sem = itertools.count(3 * CHUNKS)

    def pass_on(i):
        a, b = (low + high)[i], (high + low)[i]
        h_wait(dn, a)
        if a in low:
            h_to(up, dn, a, next(sem))
        h_to(sib, dn, a, next(sem))
        h_wait(up, b)
        if b in high:
            h_to(dn, up, b, next(sem))
        h_to(sib, up, b, next(sem))

    for i in range(CHUNKS // 2):
        pass_on(i)
    h_wait(dn_chip * 2 + 1 - core, low[0])

    for other in range(1, N_CTX):
        dev = lax.rem(me + other, N_CTX)
        go(send(docs, dall.at[me], d_send.at[other], d_recv.at[me], dev))
    dall[me] = docs[...]

    far_chips = ((opp_chip, opp), (up_chip, up), (dn_chip, dn))
    for i, (far_chip, far) in enumerate(far_chips):
        feats = pl.ds(pl.multiple_of(far_chip * HDIM, HDIM), HDIM)
        go(send(val.at[:, feats], vall.at[me], v_send.at[i], v_recv.at[me], far))
    go(send(val.at[:, kv_head], vall.at[me], v_send.at[3], v_recv.at[me], sib))
    sib_feats = pl.ds(pl.multiple_of(sib * HDIM, HDIM), HDIM)
    go(send(qry.at[:, sib_feats], qall.at[me], q_send.at[6], q_recv.at[me], sib))
    go(send(cot.at[:, sib_feats], call.at[me], c_send.at[6], c_recv.at[me], sib))
    for i, (far_chip, far) in enumerate(far_chips):
        for j in range(2):
            dev = far_chip * 2 + j
            feats = pl.ds(pl.multiple_of(dev * HDIM, HDIM), HDIM)
            go(send(qry.at[:, feats], qall.at[me], q_send.at[2 * i + j], q_recv.at[me], dev))
            go(send(cot.at[:, feats], call.at[me], c_send.at[2 * i + j], c_recv.at[me], dev))

    for copy in local_copies:
        copy.wait()

    def project(p):
        block = hall[pl.ds(2 * p, 2)].reshape(2 * ROWS, hall.shape[2])
        out = jnp.dot(block, wown[...], preferred_element_type=jnp.float32)
        rows = pl.ds(pl.multiple_of(p * 2 * ROWS, 2 * ROWS), 2 * ROWS)
        kbuf[rows, own_half] = out.astype(jnp.bfloat16)
        go(send(kbuf.at[rows, own_half], kbuf.at[rows, own_half], k_send.at[p], k_recv.at[p], sib))

    for k in range(CHUNKS):
        h_wait(sib, k)
    project(chip)

    for i in range(CHUNKS // 2, CHUNKS):
        pass_on(i)
    for k in range(CHUNKS):
        h_wait(up_chip * 2 + 1 - core, k)
    project(up_chip)
    for k in range(1, CHUNKS):
        h_wait(dn_chip * 2 + 1 - core, k)
    project(dn_chip)
    for k in low + high:
        h_wait(opp, k)
        h_to(sib, opp, k, next(sem))
    for k in range(CHUNKS):
        h_wait(opp_chip * 2 + 1 - core, k)
    project(opp_chip)

    for i, far in enumerate((up, dn, opp)):
        send(vall.at[far], vall.at[far], v_send.at[0], v_recv.at[far], sib).wait_recv()
        go(send(vall.at[far], vall.at[far], v_send.at[4 + i], v_recv.at[far], sib))
    for other in range(1, N_CTX):
        src = lax.rem(me + other, N_CTX)
        send(docs, dall.at[src], d_send.at[0], d_recv.at[src], sib).wait_recv()

    doc_rows = [dall[s] for s in range(N_CTX)]
    starts = [jnp.zeros(row.shape, jnp.float32) for row in doc_rows]
    for v in range(3):
        total = jnp.zeros((1, 1), jnp.float32)
        for row in doc_rows:
            total = total + jnp.sum(jnp.where(row == v, 1.0, 0.0), axis=1, keepdims=True)
        starts = [s + jnp.where(row > v, total, 0.0) for s, row in zip(starts, doc_rows)]
    for p in range(CHIPS):
        both = jnp.concatenate([starts[2 * p], starts[2 * p + 1]], axis=1)
        first_pos[p] = both.astype(jnp.int32)
    dkacc[...] = jnp.zeros_like(dkacc)

    for p in (chip, up_chip, dn_chip, opp_chip):
        src = 2 * p + 1 - core
        send(vall.at[src], vall.at[src], v_send.at[0], v_recv.at[src], sib).wait_recv()
        rows = pl.ds(pl.multiple_of(p * 2 * ROWS, 2 * ROWS), 2 * ROWS)
        half = kbuf.at[rows, sib_half]
        send(half, half, k_send.at[0], k_recv.at[p], sib).wait_recv()

    block = 2 * ROWS
    keys = 3 * block

    @pl.loop(0, CHIPS)
    def _(turn):
        p = lax.rem(chip + turn + (turn // 2) * (5 - 2 * turn), CHIPS)
        for j in range(2):
            src = 2 * p + j

            @pl.when(src != me)
            def _():
                send(qall.at[src], qall.at[src], q_send.at[0], q_recv.at[src], sib).wait_recv()
                send(call.at[src], call.at[src], c_send.at[0], c_recv.at[src], sib).wait_recv()

        first = p // 3
        rows = pl.ds(pl.multiple_of(first * block, block), keys)
        q = qall[pl.ds(2 * p, 2)].reshape(block, HDIM)
        c = call[pl.ds(2 * p, 2)].reshape(block, HDIM)
        v = vall[pl.ds(2 * first, 6)].reshape(keys, HDIM)
        t = jnp.tanh(nt(kbuf[rows, :], q) * (1.0 / (HDIM**0.5 * softcap)))
        key_pos = first * block + lax.broadcasted_iota(jnp.int32, (keys, block), 0)
        query_pos = p * block + lax.broadcasted_iota(jnp.int32, (keys, block), 1)
        allowed = (key_pos <= query_pos) & (key_pos >= first_pos[p])
        e = jnp.where(allowed, jnp.exp(softcap * t), 0.0)
        prob_grad = nt(v, c)
        norm = 1.0 / jnp.sum(e, axis=0, keepdims=True)
        row_dot = jnp.sum(e * prob_grad, axis=0, keepdims=True) * norm
        score_grad = (e * norm) * (prob_grad - row_dot) * (1.0 - t * t)
        dkacc[rows, :] += jnp.dot(
            score_grad.astype(jnp.bfloat16), q, preferred_element_type=jnp.float32
        )

    scale = 1.0 / HDIM**0.5
    dksend[...] = (dkacc[:, sib_half] * scale).astype(jnp.bfloat16)
    swap = send(dksend, dkrecv, g_send.at[0], g_recv.at[0], sib)
    go(swap)
    swap.wait_recv()
    dk = dkacc[:, own_half] * scale + dkrecv[...].astype(jnp.float32)
    dkown[...] = dk.T.astype(jnp.bfloat16)

    width = 512

    @pl.loop(0, grad.shape[0] // width)
    def _(i):
        cols = pl.ds(pl.multiple_of(i * width, width), width)
        h = hall[:, :, cols].reshape(N_CTX * ROWS, width)
        g = jnp.dot(dkown[...], h, preferred_element_type=jnp.float32).T
        grad[cols, :] = g.astype(jnp.bfloat16)
        stepped[cols, :] = (wown[cols, :].astype(jnp.float32) - step_size * g).astype(jnp.bfloat16)

    for copy in started:
        copy.wait_send()


def local_gradient(hidden, queries, values, cotangent, key_weight, doc_ids, round_index):
    depth = hidden.shape[1]
    dma = pltpu.SemaphoreType.DMA
    bf16, f32 = jnp.bfloat16, jnp.float32
    hbm = pl.BlockSpec(memory_space=pltpu.HBM)
    smem = pl.BlockSpec(memory_space=pltpu.SMEM)
    vmem = pl.BlockSpec(memory_space=pltpu.VMEM)
    seq = N_CTX * ROWS
    return pl.pallas_call(
        gradient_kernel,
        out_shape=[jax.ShapeDtypeStruct((depth, 128), bf16)] * 2
        + [jax.ShapeDtypeStruct((1,), jnp.int32)],
        in_specs=[hbm] * 5 + [vmem, smem],
        out_specs=[vmem, vmem, smem],
        scratch_shapes=[
            pltpu.VMEM((N_CTX, ROWS, depth), bf16),
            pltpu.VMEM((N_CTX, ROWS, HDIM), bf16),
            pltpu.VMEM((N_CTX, ROWS, HDIM), bf16),
            pltpu.VMEM((N_CTX, ROWS, HDIM), bf16),
            pltpu.VMEM((N_CTX, 1, ROWS), jnp.int32),
            pltpu.VMEM((depth, 128), bf16),
            pltpu.VMEM((seq, HDIM), bf16),
            pltpu.VMEM((seq, HDIM), f32),
            pltpu.VMEM((seq, 128), bf16),
            pltpu.VMEM((seq, 128), bf16),
            pltpu.VMEM((128, seq), bf16),
            pltpu.VMEM((CHIPS, 1, 2 * ROWS), jnp.int32),
            dma((5,)),
            dma((N_CTX, CHUNKS)),
            dma((7 * CHUNKS,)),
            dma((N_CTX,)),
            dma((7,)),
            dma((N_CTX,)),
            dma((7,)),
            dma((N_CTX,)),
            dma((7,)),
            dma((N_CTX,)),
            dma((N_CTX,)),
            dma((CHIPS,)),
            dma((CHIPS,)),
            dma((1,)),
            dma((1,)),
        ],
        compiler_params=pltpu.CompilerParams(
            collective_id=0, has_side_effects=True, vmem_limit_bytes=60 * 1024 * 1024
        ),
        name="gradient",
    )(hidden, queries, values, cotangent, key_weight, doc_ids, round_index)


def on_device(hidden, queries, values, cotangent, key_weight, doc_ids, round_index):
    gradient, stepped, mask = local_gradient(
        hidden[0], queries[0], values[0], cotangent[0], key_weight[0], doc_ids, round_index
    )
    averaged = gossip_rounds(stepped, mask[0])
    return (averaged[None], gradient[None])


def solution(mesh):
    return jax.shard_map(
        on_device,
        mesh=mesh,
        in_specs=(
            P("rep", "ctx", None),
            P("rep", "ctx", None),
            P("rep", "ctx", None),
            P("rep", "ctx", None),
            P("rep", None, "ctx"),
            P("rep", "ctx"),
            P(),
        ),
        out_specs=(P("rep", None, "ctx"), P("rep", None, "ctx")),
        check_vma=False,
    )
```

```python
import itertools
from functools import partial

import jax
import jax.numpy as jnp
from jax import lax
from jax.experimental import pallas as pl
from jax.experimental.pallas import tpu as pltpu
from jax.sharding import PartitionSpec as P

MESH = pl.DeviceIdType.MESH

HDIM = 256
HEADS = 8
KVH = 4
GOSSIP = 3
N_CTX = 8
CHIPS = 4
ROWS = 128
CHUNKS = 4
AHEAD = 2
RANKS = 6

softcap = 50.0
step_size = 0.0005


PIECES = 7
INNER = 3


def gossip_plan(bits):
    outer = tuple(bit for bit in bits if bit < INNER)
    inner = tuple(bit for bit in bits if bit >= INNER)
    if bits == (INNER, INNER + 1):
        outer, inner = bits[:1], bits[1:]
    elif not (outer and inner):
        outer, inner = (), bits
    depth = 1 if outer else 0
    if len(inner) == 1:
        plan = [("swap", inner, depth)]
    else:
        plan = [("scatter", inner, depth), ("gather", inner, depth)]
    if outer:
        plan = [("scatter", outer, 0)] + plan + [("gather", outer, 0)]
    return plan


def gossip_kernel(bits, x, out, acc, landing, send_sem, recv_sem):
    me = lax.axis_index("rep")
    plan = gossip_plan(bits)
    stages = len(plan)
    reduced = max(s for s, (kind, _, _) in enumerate(plan) if kind != "gather")
    rows = x.shape[0] // PIECES
    digit = {bit: lax.rem(me // (1 << bit), 2) for bit in bits}

    def peers(group):
        place = sum(digit[bit] << i for i, bit in enumerate(group))
        others = []
        for flip in range(1, 1 << len(group)):
            device, there = me, 0
            for i, bit in enumerate(group):
                if flip >> i & 1:
                    device = device + (1 - 2 * digit[bit]) * (1 << bit)
                    there = there + ((1 - digit[bit]) << i)
                else:
                    there = there + (digit[bit] << i)
            others.append((device, there))
        return place, others

    groups = {group: peers(group) for _, group, _ in plan}
    met = [device for _, others in groups.values() for device, _ in others]
    barrier = pltpu.get_barrier_semaphore()
    for device in met:
        pl.semaphore_signal(barrier, inc=1, device_id={"rep": device}, device_id_type=MESH)
    pl.semaphore_wait(barrier, len(met))

    def region(piece, depth):
        base, size = piece * rows, rows
        if depth:
            group = plan[0][1]
            size //= 1 << len(group)
            base = base + groups[group][0] * size
        return base, size

    def at(ref, base, size):
        return ref.at[pl.ds(pl.multiple_of(base, 16), size), :]

    def landed(stage, slot, piece, size):
        return landing.at[stage, slot, pl.ds(pl.multiple_of(piece * size, 16), size), :]

    def transfers(piece, stage, arriving=False):
        kind, group, depth = plan[stage]
        base, size = region(piece, depth)
        src = x if stage == 0 else acc
        place, others = groups[group]
        part = size if kind == "swap" else size >> len(group)
        for slot, (device, there) in enumerate(others):
            if kind == "gather":
                sent = at(out, base + place * part, part)
                dst = at(out, base + there * part, part) if arriving else sent
            else:
                sent = at(src, base if kind == "swap" else base + there * part, part)
                dst = landed(stage, slot, piece, part)
            yield pltpu.make_async_remote_copy(
                src_ref=sent, dst_ref=dst, send_sem=send_sem.at[piece, stage, slot],
                recv_sem=recv_sem.at[piece, stage, slot], device_id={"rep": device},
                device_id_type=MESH,
            )

    def start(piece, stage):
        for copy in transfers(piece, stage):
            copy.start()

    def finish(piece, stage):
        for copy in transfers(piece, stage, arriving=True):
            copy.wait_recv()
        kind, group, depth = plan[stage]
        if kind != "gather":
            base, size = region(piece, depth)
            place, others = groups[group]
            if kind == "scatter":
                size >>= len(group)
                base = base + place * size
            total = at(x if stage == 0 else acc, base, size)[...].astype(jnp.float32)
            for slot in range(len(others)):
                total = total + landed(stage, slot, piece, size)[...].astype(jnp.float32)
            mean = total * (1.0 / (1 << len(group)))
            at(out if stage == reduced else acc, base, size)[...] = mean.astype(jnp.bfloat16)

    @pl.loop(0, PIECES)
    def _(piece):
        start(piece, 0)

    for stage in range(stages):

        @pl.loop(0, PIECES)
        def _(piece, stage=stage):
            finish(piece, stage)
            if stage + 1 < stages:
                start(piece, stage + 1)

    @pl.loop(0, PIECES)
    def _(piece):
        for stage in range(stages):
            for copy in transfers(piece, stage):
                copy.wait_send()


def gossip(bits, number):
    def run(stepped):
        shape = stepped.shape
        plan = gossip_plan(bits)
        sums = [s for s, (kind, _, _) in enumerate(plan) if kind != "gather"]
        slots = max((1 << len(group)) - 1 for _, group, _ in plan)
        deepest = max(shape[0] >> (0 if kind == "swap" else len(group)) for kind, group, _ in plan)
        vmem = pl.BlockSpec(memory_space=pltpu.VMEM)
        return pl.pallas_call(
            partial(gossip_kernel, bits),
            out_shape=jax.ShapeDtypeStruct(shape, jnp.bfloat16),
            in_specs=[vmem],
            out_specs=vmem,
            scratch_shapes=[
                pltpu.VMEM(shape, jnp.bfloat16),
                pltpu.VMEM((max(sums) + 1, slots, deepest, shape[1]), jnp.bfloat16),
            ]
            + [pltpu.SemaphoreType.DMA((PIECES, len(plan), slots))] * 2,
            compiler_params=pltpu.CompilerParams(
                collective_id=number, has_side_effects=True, vmem_limit_bytes=24 * 1024 * 1024
            ),
            name="gossip",
        )(stepped)

    return run


def gossip_rounds(stepped, mask):
    branches = []
    for case in range(1 << RANKS):
        bits = tuple(bit for bit in range(RANKS) if case >> bit & 1)
        if 1 <= len(bits) <= GOSSIP:
            branches.append(gossip(bits, 1 + case))
        else:
            branches.append(lambda kept: kept)
    return lax.switch(mask, branches, stepped)


def nt(a, b):
    return lax.dot_general(a, b, (((1,), (1,)), ((), ())), preferred_element_type=jnp.float32)


def gradient_kernel(
    hid, qry, val, cot, wgt, docs, rounds, grad, stepped, mask,
    hall, qall, call, vall, dall, wown, kbuf, dkacc, dksend, dkrecv, dkown, first_pos,
    local, h_recv, h_send, q_recv, q_send, c_recv, c_send, v_recv, v_send, d_recv, d_send,
    k_recv, k_send, g_recv, g_send,
):
    me = lax.axis_index("ctx")
    chip = me // 2
    core = lax.rem(me, 2)
    sib = chip * 2 + (1 - core)
    way = 1 - 2 * lax.rem(lax.axis_index("rep"), 2)
    up_chip = lax.rem(chip + CHIPS + way, CHIPS)
    dn_chip = lax.rem(chip + CHIPS - way, CHIPS)
    opp_chip = lax.rem(chip + 2, CHIPS)
    up = up_chip * 2 + core
    dn = dn_chip * 2 + core
    opp = opp_chip * 2 + core
    rows_of = ROWS // CHUNKS

    def send(src, dst, ssem, rsem, dev):
        return pltpu.make_async_remote_copy(
            src_ref=src, dst_ref=dst, send_sem=ssem, recv_sem=rsem,
            device_id={"ctx": dev}, device_id_type=MESH,
        )

    mask[0] = (1 << rounds[0]) | (1 << rounds[1]) | (1 << rounds[2])
    barrier = pltpu.get_barrier_semaphore()
    for other in (sib, up, dn):
        pl.semaphore_signal(barrier, inc=1, device_id={"ctx": other}, device_id_type=MESH)

    head = pl.ds(pl.multiple_of(me * HDIM, HDIM), HDIM)
    kv_head = pl.ds(pl.multiple_of(chip * HDIM, HDIM), HDIM)
    own_half = pl.ds(pl.multiple_of(core * 128, 128), 128)
    sib_half = pl.ds(pl.multiple_of((1 - core) * 128, 128), 128)
    local_copies = [
        pltpu.make_async_copy(hid, hall.at[me], local.at[0]),
        pltpu.make_async_copy(wgt, wown, local.at[1]),
        pltpu.make_async_copy(qry.at[:, head], qall.at[me], local.at[2]),
        pltpu.make_async_copy(cot.at[:, head], call.at[me], local.at[3]),
        pltpu.make_async_copy(val.at[:, kv_head], vall.at[me], local.at[4]),
    ]
    for copy in local_copies:
        copy.start()
    pl.semaphore_wait(barrier, 3)

    started = []

    def go(copy):
        copy.start()
        started.append(copy)

    def piece(k):
        return pl.ds(k * rows_of, rows_of)

    low = list(range(AHEAD))
    high = list(range(AHEAD, CHUNKS))

    def h_to(dev, origin, k, sem, src=None):
        slot = hall.at[origin, piece(k), :]
        go(send(slot if src is None else src, slot, h_send.at[sem], h_recv.at[origin, k], dev))

    def h_wait(origin, k):
        slot = hall.at[origin, piece(k), :]
        send(slot, slot, h_send.at[0], h_recv.at[origin, k], sib).wait_recv()

    for a, b in zip(low + high, high + low):
        h_to(up, me, a, a, hid.at[piece(a), :])
        h_to(dn, me, b, CHUNKS + b, hid.at[piece(b), :])
    for k in range(CHUNKS):
        h_to(sib, me, k, 2 * CHUNKS + k, hid.at[piece(k), :])
    sem = itertools.count(3 * CHUNKS)

    def pass_on(i):
        a, b = (low + high)[i], (high + low)[i]
        h_wait(dn, a)
        if a in low:
            h_to(up, dn, a, next(sem))
        h_to(sib, dn, a, next(sem))
        h_wait(up, b)
        if b in high:
            h_to(dn, up, b, next(sem))
        h_to(sib, up, b, next(sem))

    for i in range(CHUNKS // 2):
        pass_on(i)
    h_wait(dn_chip * 2 + 1 - core, low[0])

    for other in range(1, N_CTX):
        dev = lax.rem(me + other, N_CTX)
        go(send(docs, dall.at[me], d_send.at[other], d_recv.at[me], dev))
    dall[me] = docs[...]

    far_chips = ((opp_chip, opp), (up_chip, up), (dn_chip, dn))
    for i, (far_chip, far) in enumerate(far_chips):
        feats = pl.ds(pl.multiple_of(far_chip * HDIM, HDIM), HDIM)
        go(send(val.at[:, feats], vall.at[me], v_send.at[i], v_recv.at[me], far))
    go(send(val.at[:, kv_head], vall.at[me], v_send.at[3], v_recv.at[me], sib))
    sib_feats = pl.ds(pl.multiple_of(sib * HDIM, HDIM), HDIM)
    go(send(qry.at[:, sib_feats], qall.at[me], q_send.at[6], q_recv.at[me], sib))
    go(send(cot.at[:, sib_feats], call.at[me], c_send.at[6], c_recv.at[me], sib))
    for i, (far_chip, far) in enumerate(far_chips):
        for j in range(2):
            dev = far_chip * 2 + j
            feats = pl.ds(pl.multiple_of(dev * HDIM, HDIM), HDIM)
            go(send(qry.at[:, feats], qall.at[me], q_send.at[2 * i + j], q_recv.at[me], dev))
            go(send(cot.at[:, feats], call.at[me], c_send.at[2 * i + j], c_recv.at[me], dev))

    for copy in local_copies:
        copy.wait()

    def project(p):
        block = hall[pl.ds(2 * p, 2)].reshape(2 * ROWS, hall.shape[2])
        out = jnp.dot(block, wown[...], preferred_element_type=jnp.float32)
        rows = pl.ds(pl.multiple_of(p * 2 * ROWS, 2 * ROWS), 2 * ROWS)
        kbuf[rows, own_half] = out.astype(jnp.bfloat16)
        go(send(kbuf.at[rows, own_half], kbuf.at[rows, own_half], k_send.at[p], k_recv.at[p], sib))

    for k in range(CHUNKS):
        h_wait(sib, k)
    project(chip)

    for i in range(CHUNKS // 2, CHUNKS):
        pass_on(i)
    for k in range(CHUNKS):
        h_wait(up_chip * 2 + 1 - core, k)
    project(up_chip)
    for k in range(1, CHUNKS):
        h_wait(dn_chip * 2 + 1 - core, k)
    project(dn_chip)
    for k in low + high:
        h_wait(opp, k)
        h_to(sib, opp, k, next(sem))
    for k in range(CHUNKS):
        h_wait(opp_chip * 2 + 1 - core, k)
    project(opp_chip)

    for i, far in enumerate((up, dn, opp)):
        send(vall.at[far], vall.at[far], v_send.at[0], v_recv.at[far], sib).wait_recv()
        go(send(vall.at[far], vall.at[far], v_send.at[4 + i], v_recv.at[far], sib))
    for other in range(1, N_CTX):
        src = lax.rem(me + other, N_CTX)
        send(docs, dall.at[src], d_send.at[0], d_recv.at[src], sib).wait_recv()

    doc_rows = [dall[s] for s in range(N_CTX)]
    starts = [jnp.zeros(row.shape, jnp.float32) for row in doc_rows]
    for v in range(3):
        total = jnp.zeros((1, 1), jnp.float32)
        for row in doc_rows:
            total = total + jnp.sum(jnp.where(row == v, 1.0, 0.0), axis=1, keepdims=True)
        starts = [s + jnp.where(row > v, total, 0.0) for s, row in zip(starts, doc_rows)]
    for p in range(CHIPS):
        both = jnp.concatenate([starts[2 * p], starts[2 * p + 1]], axis=1)
        first_pos[p] = both.astype(jnp.int32)
    dkacc[...] = jnp.zeros_like(dkacc)

    for p in (chip, up_chip, dn_chip, opp_chip):
        src = 2 * p + 1 - core
        send(vall.at[src], vall.at[src], v_send.at[0], v_recv.at[src], sib).wait_recv()
        rows = pl.ds(pl.multiple_of(p * 2 * ROWS, 2 * ROWS), 2 * ROWS)
        half = kbuf.at[rows, sib_half]
        send(half, half, k_send.at[0], k_recv.at[p], sib).wait_recv()

    block = 2 * ROWS
    keys = 3 * block

    @pl.loop(0, CHIPS)
    def _(turn):
        p = lax.rem(chip + turn + (turn // 2) * (5 - 2 * turn), CHIPS)
        for j in range(2):
            src = 2 * p + j

            @pl.when(src != me)
            def _():
                send(qall.at[src], qall.at[src], q_send.at[0], q_recv.at[src], sib).wait_recv()
                send(call.at[src], call.at[src], c_send.at[0], c_recv.at[src], sib).wait_recv()

        first = p // 3
        rows = pl.ds(pl.multiple_of(first * block, block), keys)
        q = qall[pl.ds(2 * p, 2)].reshape(block, HDIM)
        c = call[pl.ds(2 * p, 2)].reshape(block, HDIM)
        v = vall[pl.ds(2 * first, 6)].reshape(keys, HDIM)
        t = jnp.tanh(nt(kbuf[rows, :], q) * (1.0 / (HDIM**0.5 * softcap)))
        key_pos = first * block + lax.broadcasted_iota(jnp.int32, (keys, block), 0)
        query_pos = p * block + lax.broadcasted_iota(jnp.int32, (keys, block), 1)
        allowed = (key_pos <= query_pos) & (key_pos >= first_pos[p])
        e = jnp.where(allowed, jnp.exp(softcap * t), 0.0)
        prob_grad = nt(v, c)
        norm = 1.0 / jnp.sum(e, axis=0, keepdims=True)
        row_dot = jnp.sum(e * prob_grad, axis=0, keepdims=True) * norm
        score_grad = (e * norm) * (prob_grad - row_dot) * (1.0 - t * t)
        dkacc[rows, :] += jnp.dot(
            score_grad.astype(jnp.bfloat16), q, preferred_element_type=jnp.float32
        )

    scale = 1.0 / HDIM**0.5
    dksend[...] = (dkacc[:, sib_half] * scale).astype(jnp.bfloat16)
    swap = send(dksend, dkrecv, g_send.at[0], g_recv.at[0], sib)
    go(swap)
    swap.wait_recv()
    dk = dkacc[:, own_half] * scale + dkrecv[...].astype(jnp.float32)
    dkown[...] = dk.T.astype(jnp.bfloat16)

    width = 896

    @pl.loop(0, grad.shape[0] // width)
    def _(i):
        cols = pl.ds(pl.multiple_of(i * width, width), width)
        h = hall[:, :, cols].reshape(N_CTX * ROWS, width)
        g = jnp.dot(dkown[...], h, preferred_element_type=jnp.float32).T
        grad[cols, :] = g.astype(jnp.bfloat16)
        stepped[cols, :] = (wown[cols, :].astype(jnp.float32) - step_size * g).astype(jnp.bfloat16)

    for copy in started:
        copy.wait_send()


def local_gradient(hidden, queries, values, cotangent, key_weight, doc_ids, round_index):
    depth = hidden.shape[1]
    dma = pltpu.SemaphoreType.DMA
    bf16, f32 = jnp.bfloat16, jnp.float32
    hbm = pl.BlockSpec(memory_space=pltpu.HBM)
    smem = pl.BlockSpec(memory_space=pltpu.SMEM)
    vmem = pl.BlockSpec(memory_space=pltpu.VMEM)
    seq = N_CTX * ROWS
    return pl.pallas_call(
        gradient_kernel,
        out_shape=[jax.ShapeDtypeStruct((depth, 128), bf16)] * 2
        + [jax.ShapeDtypeStruct((1,), jnp.int32)],
        in_specs=[hbm] * 5 + [vmem, smem],
        out_specs=[vmem, vmem, smem],
        scratch_shapes=[
            pltpu.VMEM((N_CTX, ROWS, depth), bf16),
            pltpu.VMEM((N_CTX, ROWS, HDIM), bf16),
            pltpu.VMEM((N_CTX, ROWS, HDIM), bf16),
            pltpu.VMEM((N_CTX, ROWS, HDIM), bf16),
            pltpu.VMEM((N_CTX, 1, ROWS), jnp.int32),
            pltpu.VMEM((depth, 128), bf16),
            pltpu.VMEM((seq, HDIM), bf16),
            pltpu.VMEM((seq, HDIM), f32),
            pltpu.VMEM((seq, 128), bf16),
            pltpu.VMEM((seq, 128), bf16),
            pltpu.VMEM((128, seq), bf16),
            pltpu.VMEM((CHIPS, 1, 2 * ROWS), jnp.int32),
            dma((5,)),
            dma((N_CTX, CHUNKS)),
            dma((7 * CHUNKS,)),
            dma((N_CTX,)),
            dma((7,)),
            dma((N_CTX,)),
            dma((7,)),
            dma((N_CTX,)),
            dma((7,)),
            dma((N_CTX,)),
            dma((N_CTX,)),
            dma((CHIPS,)),
            dma((CHIPS,)),
            dma((1,)),
            dma((1,)),
        ],
        compiler_params=pltpu.CompilerParams(
            collective_id=0, has_side_effects=True, vmem_limit_bytes=60 * 1024 * 1024
        ),
        name="gradient",
    )(hidden, queries, values, cotangent, key_weight, doc_ids, round_index)


def on_device(hidden, queries, values, cotangent, key_weight, doc_ids, round_index):
    gradient, stepped, mask = local_gradient(
        hidden[0], queries[0], values[0], cotangent[0], key_weight[0], doc_ids, round_index
    )
    averaged = gossip_rounds(stepped, mask[0])
    return (averaged[None], gradient[None])


def solution(mesh):
    return jax.shard_map(
        on_device,
        mesh=mesh,
        in_specs=(
            P("rep", "ctx", None),
            P("rep", "ctx", None),
            P("rep", "ctx", None),
            P("rep", "ctx", None),
            P("rep", None, "ctx"),
            P("rep", "ctx"),
            P(),
        ),
        out_specs=(P("rep", None, "ctx"), P("rep", None, "ctx")),
        check_vma=False,
    )
```

```python
import itertools
from functools import partial

import jax
import jax.numpy as jnp
from jax import lax
from jax.experimental import pallas as pl
from jax.experimental.pallas import tpu as pltpu
from jax.sharding import PartitionSpec as P

MESH = pl.DeviceIdType.MESH

HDIM = 256
HEADS = 8
KVH = 4
GOSSIP = 3
N_CTX = 8
CHIPS = 4
ROWS = 128
CHUNKS = 4
AHEAD = 2
RANKS = 6

softcap = 50.0
step_size = 0.0005


PIECES = 7
INNER = 3


def gossip_plan(bits):
    outer = tuple(bit for bit in bits if bit < INNER)
    inner = tuple(bit for bit in bits if bit >= INNER)
    if bits == (INNER, INNER + 1):
        outer, inner = bits[:1], bits[1:]
    elif not (outer and inner):
        outer, inner = (), bits
    depth = 1 if outer else 0
    if len(inner) == 1:
        plan = [("swap", inner, depth)]
    else:
        plan = [("scatter", inner, depth), ("gather", inner, depth)]
    if outer:
        plan = [("scatter", outer, 0)] + plan + [("gather", outer, 0)]
    return plan


def gossip_kernel(bits, x, out, acc, landing, send_sem, recv_sem):
    me = lax.axis_index("rep")
    plan = gossip_plan(bits)
    stages = len(plan)
    reduced = max(s for s, (kind, _, _) in enumerate(plan) if kind != "gather")
    rows = x.shape[0] // PIECES
    digit = {bit: lax.rem(me // (1 << bit), 2) for bit in bits}

    def peers(group):
        place = sum(digit[bit] << i for i, bit in enumerate(group))
        others = []
        for flip in range(1, 1 << len(group)):
            device, there = me, 0
            for i, bit in enumerate(group):
                if flip >> i & 1:
                    device = device + (1 - 2 * digit[bit]) * (1 << bit)
                    there = there + ((1 - digit[bit]) << i)
                else:
                    there = there + (digit[bit] << i)
            others.append((device, there))
        return place, others

    groups = {group: peers(group) for _, group, _ in plan}
    met = [device for _, others in groups.values() for device, _ in others]
    barrier = pltpu.get_barrier_semaphore()
    for device in met:
        pl.semaphore_signal(barrier, inc=1, device_id={"rep": device}, device_id_type=MESH)
    pl.semaphore_wait(barrier, len(met))

    def region(piece, depth):
        base, size = piece * rows, rows
        if depth:
            group = plan[0][1]
            size //= 1 << len(group)
            base = base + groups[group][0] * size
        return base, size

    def at(ref, base, size):
        return ref.at[pl.ds(pl.multiple_of(base, 16), size), :]

    def landed(stage, slot, piece, size):
        return landing.at[stage, slot, pl.ds(pl.multiple_of(piece * size, 16), size), :]

    def transfers(piece, stage, arriving=False):
        kind, group, depth = plan[stage]
        base, size = region(piece, depth)
        src = x if stage == 0 else acc
        place, others = groups[group]
        part = size if kind == "swap" else size >> len(group)
        for slot, (device, there) in enumerate(others):
            if kind == "gather":
                sent = at(out, base + place * part, part)
                dst = at(out, base + there * part, part) if arriving else sent
            else:
                sent = at(src, base if kind == "swap" else base + there * part, part)
                dst = landed(stage, slot, piece, part)
            yield pltpu.make_async_remote_copy(
                src_ref=sent, dst_ref=dst, send_sem=send_sem.at[piece, stage, slot],
                recv_sem=recv_sem.at[piece, stage, slot], device_id={"rep": device},
                device_id_type=MESH,
            )

    def start(piece, stage):
        for copy in transfers(piece, stage):
            copy.start()

    def finish(piece, stage):
        for copy in transfers(piece, stage, arriving=True):
            copy.wait_recv()
        kind, group, depth = plan[stage]
        if kind != "gather":
            base, size = region(piece, depth)
            place, others = groups[group]
            if kind == "scatter":
                size >>= len(group)
                base = base + place * size
            total = at(x if stage == 0 else acc, base, size)[...].astype(jnp.float32)
            for slot in range(len(others)):
                total = total + landed(stage, slot, piece, size)[...].astype(jnp.float32)
            mean = total * (1.0 / (1 << len(group)))
            at(out if stage == reduced else acc, base, size)[...] = mean.astype(jnp.bfloat16)

    @pl.loop(0, PIECES)
    def _(piece):
        start(piece, 0)

    for stage in range(stages):

        @pl.loop(0, PIECES)
        def _(piece, stage=stage):
            finish(piece, stage)
            if stage + 1 < stages:
                start(piece, stage + 1)

    @pl.loop(0, PIECES)
    def _(piece):
        for stage in range(stages):
            for copy in transfers(piece, stage):
                copy.wait_send()


def gossip(bits, number):
    def run(stepped):
        shape = stepped.shape
        plan = gossip_plan(bits)
        sums = [s for s, (kind, _, _) in enumerate(plan) if kind != "gather"]
        slots = max((1 << len(group)) - 1 for _, group, _ in plan)
        deepest = max(shape[0] >> (0 if kind == "swap" else len(group)) for kind, group, _ in plan)
        vmem = pl.BlockSpec(memory_space=pltpu.VMEM)
        return pl.pallas_call(
            partial(gossip_kernel, bits),
            out_shape=jax.ShapeDtypeStruct(shape, jnp.bfloat16),
            in_specs=[vmem],
            out_specs=vmem,
            scratch_shapes=[
                pltpu.VMEM(shape, jnp.bfloat16),
                pltpu.VMEM((max(sums) + 1, slots, deepest, shape[1]), jnp.bfloat16),
            ]
            + [pltpu.SemaphoreType.DMA((PIECES, len(plan), slots))] * 2,
            compiler_params=pltpu.CompilerParams(
                collective_id=number, has_side_effects=True, vmem_limit_bytes=24 * 1024 * 1024
            ),
            name="gossip",
        )(stepped)

    return run


def gossip_rounds(stepped, mask):
    branches = []
    for case in range(1 << RANKS):
        bits = tuple(bit for bit in range(RANKS) if case >> bit & 1)
        if 1 <= len(bits) <= GOSSIP:
            branches.append(gossip(bits, 1 + case))
        else:
            branches.append(lambda kept: kept)
    return lax.switch(mask, branches, stepped)


def nt(a, b):
    return lax.dot_general(a, b, (((1,), (1,)), ((), ())), preferred_element_type=jnp.float32)


def gradient_kernel(
    hid, qry, val, cot, wgt, docs, rounds, grad, stepped, mask,
    hall, qall, call, vall, dall, wown, kbuf, dkacc, dksend, dkrecv, dkown, first_pos,
    local, h_recv, h_send, q_recv, q_send, c_recv, c_send, v_recv, v_send, d_recv, d_send,
    k_recv, k_send, g_recv, g_send,
):
    me = lax.axis_index("ctx")
    chip = me // 2
    core = lax.rem(me, 2)
    sib = chip * 2 + (1 - core)
    way = 1 - 2 * lax.rem(lax.axis_index("rep"), 2)
    up_chip = lax.rem(chip + CHIPS + way, CHIPS)
    dn_chip = lax.rem(chip + CHIPS - way, CHIPS)
    opp_chip = lax.rem(chip + 2, CHIPS)
    up = up_chip * 2 + core
    dn = dn_chip * 2 + core
    opp = opp_chip * 2 + core
    rows_of = ROWS // CHUNKS

    def send(src, dst, ssem, rsem, dev):
        return pltpu.make_async_remote_copy(
            src_ref=src, dst_ref=dst, send_sem=ssem, recv_sem=rsem,
            device_id={"ctx": dev}, device_id_type=MESH,
        )

    mask[0] = (1 << rounds[0]) | (1 << rounds[1]) | (1 << rounds[2])
    barrier = pltpu.get_barrier_semaphore()
    for other in (sib, up, dn):
        pl.semaphore_signal(barrier, inc=1, device_id={"ctx": other}, device_id_type=MESH)

    head = pl.ds(pl.multiple_of(me * HDIM, HDIM), HDIM)
    kv_head = pl.ds(pl.multiple_of(chip * HDIM, HDIM), HDIM)
    own_half = pl.ds(pl.multiple_of(core * 128, 128), 128)
    sib_half = pl.ds(pl.multiple_of((1 - core) * 128, 128), 128)
    local_copies = [
        pltpu.make_async_copy(hid, hall.at[me], local.at[0]),
        pltpu.make_async_copy(wgt, wown, local.at[1]),
        pltpu.make_async_copy(qry.at[:, head], qall.at[me], local.at[2]),
        pltpu.make_async_copy(cot.at[:, head], call.at[me], local.at[3]),
        pltpu.make_async_copy(val.at[:, kv_head], vall.at[me], local.at[4]),
    ]
    for copy in local_copies:
        copy.start()
    pl.semaphore_wait(barrier, 3)

    started = []

    def go(copy):
        copy.start()
        started.append(copy)

    def piece(k):
        return pl.ds(k * rows_of, rows_of)

    low = list(range(AHEAD))
    high = list(range(AHEAD, CHUNKS))

    def h_to(dev, origin, k, sem, src=None):
        slot = hall.at[origin, piece(k), :]
        go(send(slot if src is None else src, slot, h_send.at[sem], h_recv.at[origin, k], dev))

    def h_wait(origin, k):
        slot = hall.at[origin, piece(k), :]
        send(slot, slot, h_send.at[0], h_recv.at[origin, k], sib).wait_recv()

    for a, b in zip(low + high, high + low):
        h_to(up, me, a, a, hid.at[piece(a), :])
        h_to(dn, me, b, CHUNKS + b, hid.at[piece(b), :])
    for k in range(CHUNKS):
        h_to(sib, me, k, 2 * CHUNKS + k, hid.at[piece(k), :])
    sem = itertools.count(3 * CHUNKS)

    def pass_on(i):
        a, b = (low + high)[i], (high + low)[i]
        h_wait(dn, a)
        if a in low:
            h_to(up, dn, a, next(sem))
        h_to(sib, dn, a, next(sem))
        h_wait(up, b)
        if b in high:
            h_to(dn, up, b, next(sem))
        h_to(sib, up, b, next(sem))

    for i in range(CHUNKS // 2):
        pass_on(i)
    h_wait(dn_chip * 2 + 1 - core, low[0])

    for other in range(1, N_CTX):
        dev = lax.rem(me + other, N_CTX)
        go(send(docs, dall.at[me], d_send.at[other], d_recv.at[me], dev))
    dall[me] = docs[...]

    far_chips = ((opp_chip, opp), (up_chip, up), (dn_chip, dn))
    for i, (far_chip, far) in enumerate(far_chips):
        feats = pl.ds(pl.multiple_of(far_chip * HDIM, HDIM), HDIM)
        go(send(val.at[:, feats], vall.at[me], v_send.at[i], v_recv.at[me], far))
    go(send(val.at[:, kv_head], vall.at[me], v_send.at[3], v_recv.at[me], sib))
    sib_feats = pl.ds(pl.multiple_of(sib * HDIM, HDIM), HDIM)
    go(send(qry.at[:, sib_feats], qall.at[me], q_send.at[6], q_recv.at[me], sib))
    go(send(cot.at[:, sib_feats], call.at[me], c_send.at[6], c_recv.at[me], sib))
    for i, (far_chip, far) in enumerate(far_chips):
        for j in range(2):
            dev = far_chip * 2 + j
            feats = pl.ds(pl.multiple_of(dev * HDIM, HDIM), HDIM)
            go(send(qry.at[:, feats], qall.at[me], q_send.at[2 * i + j], q_recv.at[me], dev))
            go(send(cot.at[:, feats], call.at[me], c_send.at[2 * i + j], c_recv.at[me], dev))

    for copy in local_copies:
        copy.wait()

    def project(p):
        block = hall[pl.ds(2 * p, 2)].reshape(2 * ROWS, hall.shape[2])
        out = jnp.dot(block, wown[...], preferred_element_type=jnp.float32)
        rows = pl.ds(pl.multiple_of(p * 2 * ROWS, 2 * ROWS), 2 * ROWS)
        kbuf[rows, own_half] = out.astype(jnp.bfloat16)
        go(send(kbuf.at[rows, own_half], kbuf.at[rows, own_half], k_send.at[p], k_recv.at[p], sib))

    for k in range(CHUNKS):
        h_wait(sib, k)
    project(chip)

    for i in range(CHUNKS // 2, CHUNKS):
        pass_on(i)
    for k in range(CHUNKS):
        h_wait(up_chip * 2 + 1 - core, k)
    project(up_chip)
    for k in range(1, CHUNKS):
        h_wait(dn_chip * 2 + 1 - core, k)
    project(dn_chip)
    for k in low + high:
        h_wait(opp, k)
        h_to(sib, opp, k, next(sem))
    for k in range(CHUNKS):
        h_wait(opp_chip * 2 + 1 - core, k)
    project(opp_chip)

    for i, far in enumerate((up, dn, opp)):
        send(vall.at[far], vall.at[far], v_send.at[0], v_recv.at[far], sib).wait_recv()
        go(send(vall.at[far], vall.at[far], v_send.at[4 + i], v_recv.at[far], sib))
    for other in range(1, N_CTX):
        src = lax.rem(me + other, N_CTX)
        send(docs, dall.at[src], d_send.at[0], d_recv.at[src], sib).wait_recv()

    doc_rows = [dall[s] for s in range(N_CTX)]
    starts = [jnp.zeros(row.shape, jnp.float32) for row in doc_rows]
    for v in range(3):
        total = jnp.zeros((1, 1), jnp.float32)
        for row in doc_rows:
            total = total + jnp.sum(jnp.where(row == v, 1.0, 0.0), axis=1, keepdims=True)
        starts = [s + jnp.where(row > v, total, 0.0) for s, row in zip(starts, doc_rows)]
    for p in range(CHIPS):
        both = jnp.concatenate([starts[2 * p], starts[2 * p + 1]], axis=1)
        first_pos[p] = both.astype(jnp.int32)
    dkacc[...] = jnp.zeros_like(dkacc)

    for p in (chip, up_chip, dn_chip, opp_chip):
        src = 2 * p + 1 - core
        send(vall.at[src], vall.at[src], v_send.at[0], v_recv.at[src], sib).wait_recv()
        rows = pl.ds(pl.multiple_of(p * 2 * ROWS, 2 * ROWS), 2 * ROWS)
        half = kbuf.at[rows, sib_half]
        send(half, half, k_send.at[0], k_recv.at[p], sib).wait_recv()

    block = 2 * ROWS
    keys = 3 * block

    @pl.loop(0, CHIPS)
    def _(turn):
        p = lax.rem(chip + turn + (turn // 2) * (5 - 2 * turn), CHIPS)
        for j in range(2):
            src = 2 * p + j

            @pl.when(src != me)
            def _():
                send(qall.at[src], qall.at[src], q_send.at[0], q_recv.at[src], sib).wait_recv()
                send(call.at[src], call.at[src], c_send.at[0], c_recv.at[src], sib).wait_recv()

        first = p // 3
        rows = pl.ds(pl.multiple_of(first * block, block), keys)
        q = qall[pl.ds(2 * p, 2)].reshape(block, HDIM)
        c = call[pl.ds(2 * p, 2)].reshape(block, HDIM)
        v = vall[pl.ds(2 * first, 6)].reshape(keys, HDIM)
        t = jnp.tanh(nt(kbuf[rows, :], q) * (1.0 / (HDIM**0.5 * softcap)))
        key_pos = first * block + lax.broadcasted_iota(jnp.int32, (keys, block), 0)
        query_pos = p * block + lax.broadcasted_iota(jnp.int32, (keys, block), 1)
        allowed = (key_pos <= query_pos) & (key_pos >= first_pos[p])
        e = jnp.where(allowed, jnp.exp(softcap * t), 0.0)
        prob_grad = nt(v, c)
        norm = 1.0 / jnp.sum(e, axis=0, keepdims=True)
        row_dot = jnp.sum(e * prob_grad, axis=0, keepdims=True) * norm
        score_grad = (e * norm) * (prob_grad - row_dot) * (1.0 - t * t)
        dkacc[rows, :] += jnp.dot(
            score_grad.astype(jnp.bfloat16), q, preferred_element_type=jnp.float32
        )

    scale = 1.0 / HDIM**0.5
    dksend[...] = (dkacc[:, sib_half] * scale).astype(jnp.bfloat16)
    swap = send(dksend, dkrecv, g_send.at[0], g_recv.at[0], sib)
    go(swap)
    swap.wait_recv()
    dk = dkacc[:, own_half] * scale + dkrecv[...].astype(jnp.float32)
    dkown[...] = dk.T.astype(jnp.bfloat16)

    width = 1792

    @pl.loop(0, grad.shape[0] // width)
    def _(i):
        cols = pl.ds(pl.multiple_of(i * width, width), width)
        h = hall[:, :, cols].reshape(N_CTX * ROWS, width)
        g = jnp.dot(dkown[...], h, preferred_element_type=jnp.float32).T
        grad[cols, :] = g.astype(jnp.bfloat16)
        stepped[cols, :] = (wown[cols, :].astype(jnp.float32) - step_size * g).astype(jnp.bfloat16)

    for copy in started:
        copy.wait_send()


def local_gradient(hidden, queries, values, cotangent, key_weight, doc_ids, round_index):
    depth = hidden.shape[1]
    dma = pltpu.SemaphoreType.DMA
    bf16, f32 = jnp.bfloat16, jnp.float32
    hbm = pl.BlockSpec(memory_space=pltpu.HBM)
    smem = pl.BlockSpec(memory_space=pltpu.SMEM)
    vmem = pl.BlockSpec(memory_space=pltpu.VMEM)
    seq = N_CTX * ROWS
    return pl.pallas_call(
        gradient_kernel,
        out_shape=[jax.ShapeDtypeStruct((depth, 128), bf16)] * 2
        + [jax.ShapeDtypeStruct((1,), jnp.int32)],
        in_specs=[hbm] * 5 + [vmem, smem],
        out_specs=[vmem, vmem, smem],
        scratch_shapes=[
            pltpu.VMEM((N_CTX, ROWS, depth), bf16),
            pltpu.VMEM((N_CTX, ROWS, HDIM), bf16),
            pltpu.VMEM((N_CTX, ROWS, HDIM), bf16),
            pltpu.VMEM((N_CTX, ROWS, HDIM), bf16),
            pltpu.VMEM((N_CTX, 1, ROWS), jnp.int32),
            pltpu.VMEM((depth, 128), bf16),
            pltpu.VMEM((seq, HDIM), bf16),
            pltpu.VMEM((seq, HDIM), f32),
            pltpu.VMEM((seq, 128), bf16),
            pltpu.VMEM((seq, 128), bf16),
            pltpu.VMEM((128, seq), bf16),
            pltpu.VMEM((CHIPS, 1, 2 * ROWS), jnp.int32),
            dma((5,)),
            dma((N_CTX, CHUNKS)),
            dma((7 * CHUNKS,)),
            dma((N_CTX,)),
            dma((7,)),
            dma((N_CTX,)),
            dma((7,)),
            dma((N_CTX,)),
            dma((7,)),
            dma((N_CTX,)),
            dma((N_CTX,)),
            dma((CHIPS,)),
            dma((CHIPS,)),
            dma((1,)),
            dma((1,)),
        ],
        compiler_params=pltpu.CompilerParams(
            collective_id=0, has_side_effects=True, vmem_limit_bytes=60 * 1024 * 1024
        ),
        name="gradient",
    )(hidden, queries, values, cotangent, key_weight, doc_ids, round_index)


def on_device(hidden, queries, values, cotangent, key_weight, doc_ids, round_index):
    gradient, stepped, mask = local_gradient(
        hidden[0], queries[0], values[0], cotangent[0], key_weight[0], doc_ids, round_index
    )
    averaged = gossip_rounds(stepped, mask[0])
    return (averaged[None], gradient[None])


def solution(mesh):
    return jax.shard_map(
        on_device,
        mesh=mesh,
        in_specs=(
            P("rep", "ctx", None),
            P("rep", "ctx", None),
            P("rep", "ctx", None),
            P("rep", "ctx", None),
            P("rep", None, "ctx"),
            P("rep", "ctx"),
            P(),
        ),
        out_specs=(P("rep", None, "ctx"), P("rep", None, "ctx")),
        check_vma=False,
    )
```
